256 devices in a mesh: node: 4 (over x), rail: 64 (over z, y, core).
Axes of the slice: x: 4, y: 4, z: 8, core: 2. Of those that a mesh axis runs over, the one named last changes fastest.
Arguments:
- queries: bfloat16 [16384, 4096], P(('rail', 'node')), may hold values from -6 to 6, as said below
- keys: bfloat16 [16384, 512], P(('rail', 'node')), may hold values from -6 to 6, as said below
- values: bfloat16 [16384, 512], P(('rail', 'node')), may hold values from -6 to 6
- output_cotangent: bfloat16 [16384, 4096], P(('rail', 'node')), may hold values from -6 to 6
- doc_lengths: int32 [16], replicated, may hold values from 1 to 2048, 16384 in all
- span_slot: int32 [128], replicated, may hold values from 0 to 127, each once
Outputs:
- d_queries: bfloat16 [16384, 4096], P(('rail', 'node'))
- keys_gradient: bfloat16 [16384, 512], P(('rail', 'node'))
- values_gradient: bfloat16 [16384, 512], P(('rail', 'node'))
The draws below stay inside these ranges and needn't reach their ends.
Inputs may be any that keep to these rules, and one draw needn't show every extreme that they name: queries lie within this range in every draw. keys lie within this range in every draw. `span_slot`: a permutation of the slots.
All inputs are finite; a program needn't handle non-finite values.
Results may differ from the reference program's by a relative error of at most 0.0075.
Values may be sent and summed in bfloat16 or wider, within the bound.
A program may use at most 128 MiB of HBM per device.

```python
import math
import jax
import jax.numpy as jnp
import numpy as np
from jax import lax

QUERY_HEADS = 32
KEY_VALUE_HEADS = 4
HEAD_SIZE = 128
QUERY_GROUP = 8
NDOCS = 16
SEQUENCE_TOKENS = 16384
SPAN = 128
DOCUMENT_LIMIT = 2048
N_RAIL = 64


def draw_queries(key, part):
    key = jax.random.fold_in(key, 11)
    start_offset = jnp.clip(jax.random.normal(key, (SEQUENCE_TOKENS, QUERY_HEADS * HEAD_SIZE), jnp.float32), -5.5, 5.5)
    return start_offset.astype(jnp.bfloat16)


def draw_keys(key, part):
    key = jax.random.fold_in(key, 12)
    start_offset = jnp.clip(jax.random.normal(key, (SEQUENCE_TOKENS, KEY_VALUE_HEADS * HEAD_SIZE), jnp.float32), -5.5, 5.5)
    return start_offset.astype(jnp.bfloat16)


def shard_levels(rng, shape, pieces, low, largest):
    gain = 1.0
    for dim, parts in pieces:
        draws = jax.random.uniform(jax.random.fold_in(jax.random.fold_in(rng, 6), dim), (parts,), jnp.float32, low / len(pieces), largest / len(pieces))
        gain = gain * jnp.repeat(jnp.exp(draws), shape[dim] // parts).reshape((-1,) + (1,) * (len(shape) - 1 - dim))
    return gain


def profile(amount, total, limit, slope):
    loads = [(1 << 20) // math.isqrt(rank ** slope) + 1 for rank in range(2, amount + 1)]
    surplus, given = total - limit - (amount - 1), [1] * (amount - 1)
    while surplus > 0:
        free = [i for i in range(amount - 1) if given[i] < limit]
        mass, left = sum([loads[i] for i in free]), surplus
        for i in free:
            addition = min(limit - given[i], max(1, left * loads[i] // mass), surplus)
            given[i] = given[i] + addition
            surplus = surplus - addition
    return np.array([limit] + given)


def uneven(rng, count, total, bound, skew):
    if count == 2:
        one = jax.random.randint(rng, (), max(1, total - bound), min(bound, total - 1) + 1)
        return jnp.stack([one, total - one])
    lengths = jnp.asarray(profile(count, total, bound, skew), jnp.int32)
    twos = (count - 1) // 2
    donor, sink = lengths[1:1 + 2 * twos:2], lengths[2:2 + 2 * twos:2]
    slack = jnp.minimum(donor - 1, bound - sink)
    shifted = jax.random.randint(jax.random.fold_in(rng, 1), (twos,), 0, 1 << 20) % (slack + 1)
    lengths = lengths.at[1:1 + 2 * twos:2].set(donor - shifted).at[2:2 + 2 * twos:2].set(sink + shifted)
    return lengths[jax.random.permutation(jax.random.fold_in(rng, 2), count)]


def noise(key, dims, scale, most, shards=(), held_as=jnp.bfloat16):
    result = scale * jax.random.normal(key, dims, jnp.float32)
    if shards:
        result = result * shard_levels(key, dims, shards, -0.22, 0.18)
    return jnp.clip(result, -most, most).astype(held_as)


def setup_inputs(seed: int = 0) -> dict:
    key_list = jax.random.split(jax.random.key(seed), 7)
    return {
        "queries": draw_queries(jax.random.fold_in(key_list[6], 71), 0),
        "keys": draw_keys(jax.random.fold_in(key_list[6], 71), 0),
        "values": noise(key_list[2], (SEQUENCE_TOKENS, KEY_VALUE_HEADS * HEAD_SIZE), 1.0, 6.0, ((0, 256),)),
        "output_cotangent": noise(key_list[3], (SEQUENCE_TOKENS, QUERY_HEADS * HEAD_SIZE), 1.0, 6.0, ((0, 256),)),
        "doc_lengths": uneven(key_list[4], NDOCS, SEQUENCE_TOKENS, DOCUMENT_LIMIT, 2).astype(jnp.int32),
        "span_slot": jax.random.permutation(key_list[5], 2 * N_RAIL).astype(jnp.int32),
    }


def slot_spans(span_slot):
    slot_count = span_slot.shape[0]
    numbers = jnp.arange(slot_count, dtype=jnp.int32)
    return lax.optimization_barrier(jnp.sum(jnp.where(span_slot[:, None] == numbers[None, :], numbers[:, None], 0), axis=0)).astype(jnp.int32)

def doc_number(places, doc_ends):
    return lax.optimization_barrier(jnp.sum((places[:, None] >= doc_ends[None, :]).astype(jnp.int32), axis=1)).astype(jnp.int32)

def reference(queries, keys, values, output_cotangent, doc_lengths, span_slot):
    softmax_scale = 1.0 / math.sqrt(HEAD_SIZE)
    block_rows = min(512, SEQUENCE_TOKENS)
    win_rows = DOCUMENT_LIMIT + block_rows
    row_ids = jnp.arange(SEQUENCE_TOKENS, dtype=jnp.int32)
    span_of_slot = slot_spans(span_slot)
    row_placement = span_of_slot[row_ids // SPAN] * SPAN + row_ids % SPAN
    placement_row = span_slot[row_ids // SPAN] * SPAN + row_ids % SPAN
    doc_ends = jnp.cumsum(doc_lengths).astype(jnp.int32)
    place_doc = doc_number(row_ids, doc_ends)
    queries_sorted = queries[placement_row].reshape(SEQUENCE_TOKENS, KEY_VALUE_HEADS, QUERY_GROUP, HEAD_SIZE)
    output_sorted = output_cotangent[placement_row].reshape(SEQUENCE_TOKENS, KEY_VALUE_HEADS, QUERY_GROUP, HEAD_SIZE)
    keys_padded = jnp.concatenate([jnp.zeros((DOCUMENT_LIMIT, KEY_VALUE_HEADS * HEAD_SIZE), keys.dtype), keys[placement_row]], axis=0).reshape(DOCUMENT_LIMIT + SEQUENCE_TOKENS, KEY_VALUE_HEADS, HEAD_SIZE)
    values_padded = jnp.concatenate([jnp.zeros((DOCUMENT_LIMIT, KEY_VALUE_HEADS * HEAD_SIZE), values.dtype), values[placement_row]], axis=0).reshape(DOCUMENT_LIMIT + SEQUENCE_TOKENS, KEY_VALUE_HEADS, HEAD_SIZE)
    doc_padded = jnp.concatenate([jnp.full((DOCUMENT_LIMIT,), -1, jnp.int32), place_doc])
    place_padded = jnp.arange(DOCUMENT_LIMIT + SEQUENCE_TOKENS, dtype=jnp.int32) - DOCUMENT_LIMIT
    zeroed_gradient = jnp.zeros((DOCUMENT_LIMIT + SEQUENCE_TOKENS, KEY_VALUE_HEADS, HEAD_SIZE), jnp.float32)

    def one_block(current, block_id):
        key_gradient_local, value_gradient_local = current
        first_row = block_id * block_rows
        query_blk = lax.dynamic_slice_in_dim(queries_sorted, first_row, block_rows, 0).astype(jnp.float32)
        grad_blk = lax.dynamic_slice_in_dim(output_sorted, first_row, block_rows, 0).astype(jnp.float32)
        query_places = first_row + jnp.arange(block_rows, dtype=jnp.int32)
        query_docs = lax.dynamic_slice_in_dim(place_doc, first_row, block_rows, 0)
        key_win = lax.dynamic_slice_in_dim(keys_padded, first_row, win_rows, 0).astype(jnp.float32)
        value_win = lax.dynamic_slice_in_dim(values_padded, first_row, win_rows, 0).astype(jnp.float32)
        win_docs = lax.dynamic_slice_in_dim(doc_padded, first_row, win_rows, 0)
        win_places = lax.dynamic_slice_in_dim(place_padded, first_row, win_rows, 0)
        allowed = (win_docs[None, :] == query_docs[:, None]) & (win_places[None, :] <= query_places[:, None])
        scores = jnp.einsum('qhgd,khd->hgqk', query_blk, key_win) * softmax_scale
        scores = jnp.where(allowed[None, None], scores, -jnp.inf)
        row_max = lax.optimization_barrier(jnp.max(scores, axis=-1, keepdims=True))
        log_total = row_max + jnp.log(lax.optimization_barrier(jnp.sum(jnp.exp(scores - row_max), axis=-1, keepdims=True)))
        probs = jnp.exp(scores - log_total)
        d_probs = jnp.einsum('qhgd,khd->hgqk', grad_blk, value_win)
        row_dots = lax.optimization_barrier(jnp.sum(probs * d_probs, axis=-1, keepdims=True))
        d_scores = probs * (d_probs - row_dots)
        probs_b = lax.optimization_barrier(probs.astype(jnp.bfloat16)).astype(jnp.float32)
        d_scores_b = lax.optimization_barrier(d_scores.astype(jnp.bfloat16)).astype(jnp.float32)
        query_grad = (jnp.einsum('hgqk,khd->qhgd', d_scores_b, key_win) * softmax_scale).astype(jnp.bfloat16)
        key_part = jnp.einsum('hgqk,qhgd->khd', d_scores_b, query_blk) * softmax_scale
        value_part = jnp.einsum('hgqk,qhgd->khd', probs_b, grad_blk)
        key_gradient_local = lax.dynamic_update_slice_in_dim(key_gradient_local, lax.dynamic_slice_in_dim(key_gradient_local, first_row, win_rows, 0) + key_part, first_row, 0)
        value_gradient_local = lax.dynamic_update_slice_in_dim(value_gradient_local, lax.dynamic_slice_in_dim(value_gradient_local, first_row, win_rows, 0) + value_part, first_row, 0)
        return ((key_gradient_local, value_gradient_local), query_grad.reshape(block_rows, QUERY_HEADS * HEAD_SIZE))
    block_ids = jnp.arange(SEQUENCE_TOKENS // block_rows, dtype=jnp.int32)
    (key_gradient_local, value_gradient_local), query_blocks = lax.scan(one_block, (zeroed_gradient, zeroed_gradient), block_ids)
    d_queries = query_blocks.reshape(SEQUENCE_TOKENS, QUERY_HEADS * HEAD_SIZE)[row_placement]
    keys_gradient = key_gradient_local[DOCUMENT_LIMIT:].reshape(SEQUENCE_TOKENS, KEY_VALUE_HEADS * HEAD_SIZE)[row_placement].astype(jnp.bfloat16)
    values_gradient = value_gradient_local[DOCUMENT_LIMIT:].reshape(SEQUENCE_TOKENS, KEY_VALUE_HEADS * HEAD_SIZE)[row_placement].astype(jnp.bfloat16)
    return (d_queries, keys_gradient, values_gradient)
```

```python
import functools
import math

import jax
import jax.numpy as jnp
from jax import lax
from jax.experimental import pallas as pl
from jax.experimental.pallas import tpu as pltpu
from jax.sharding import PartitionSpec as P

HEAD = 128
SPAN = 128
NX, NZ, NY, NC = 4, 8, 4, 2
ROWS = 64
BLOCK = NX * ROWS
SLOTS = 4
QHEADS = 4
LANES = QHEADS * SPAN
TILES = 17
CUT = 160
SCALE = 1.0 / math.sqrt(HEAD)
LOG2E = 1.4426950408889634
NEG = -1e30
MESH = pl.DeviceIdType.MESH
F32 = jnp.float32
BF16 = jnp.bfloat16


def halves(lo, hi):
    mid = lo + (hi - lo) // 32 * 16
    return (lo, mid), (mid, hi)


class Place:
    def __init__(self):
        self.x = lax.axis_index("node")
        rail = lax.axis_index("rail")
        self.c = rail % NC
        self.y = (rail // NC) % NY
        self.z = rail // (NC * NY)

    def at(self, x=None, z=None, y=None, c=None):
        x = self.x if x is None else x
        z = self.z if z is None else z
        y = self.y if y is None else y
        c = self.c if c is None else c
        return (x, (z * NY + y) * NC + c)

    def ring(self, axis, step):
        if axis == "z":
            return self.at(z=(self.z + step + NZ) % NZ)
        return self.at(y=(self.y + step + NY) % NY)

    def sibling(self):
        return self.at(c=1 - self.c)

    def team(self):
        out = []
        for step in range(1, NX * NC):
            j = (self.x * NC + self.c + step) % (NX * NC)
            out.append((j, self.at(x=j // NC, c=j % NC)))
        return out


def greet(place):
    barrier = pltpu.get_barrier_semaphore()
    peers = [dev for _, dev in place.team()]
    peers += [place.ring("z", 1), place.ring("z", -1), place.ring("y", 1), place.ring("y", -1)]
    for dev in peers:
        pl.semaphore_signal(barrier, inc=1, device_id=dev, device_id_type=MESH)
    pl.semaphore_wait(barrier, len(peers))


class Copies:
    def __init__(self, send, recv):
        self.send, self.recv, self.count, self.open = send, recv, 0, []

    def make(self, src, dst, dev):
        i = self.count
        self.count += 1
        copy = pltpu.make_async_remote_copy(
            src_ref=src, dst_ref=dst, send_sem=self.send.at[i], recv_sem=self.recv.at[i],
            device_id=dev, device_id_type=MESH,
        )
        copy.start()
        self.open.append(copy)
        return copy

    def finish(self):
        for copy in self.open:
            copy.wait_send()


N_GATHER = 96


def gather_kernel(q_ref, o_ref, k_ref, v_ref, qm_ref, om_ref, kv_ref, send, recv, local):
    me = Place()
    cp = Copies(send, recv)
    greet(me)
    x, z, y, c = me.x, me.z, me.y, me.c
    j_me = x * NC + c
    wide = QHEADS * HEAD

    own = []
    kvx = []
    for step in range(1, NX):
        to = (x + step) % NX
        for i, ref in enumerate((k_ref, v_ref)):
            kvx.append(cp.make(
                ref.at[:, pl.ds(pl.multiple_of(to * HEAD, HEAD), HEAD)],
                kv_ref.at[z, y, c, i, pl.ds(pl.multiple_of(x * ROWS, ROWS), ROWS), :],
                me.at(x=to),
            ))
    for i, ref in enumerate((k_ref, v_ref)):
        own.append(pltpu.make_async_copy(
            ref.at[:, pl.ds(pl.multiple_of(x * HEAD, HEAD), HEAD)],
            kv_ref.at[z, y, c, i, pl.ds(pl.multiple_of(x * ROWS, ROWS), ROWS), :],
            local.at[i],
        ))
        own[-1].start()
    rows = pl.ds(pl.multiple_of(c * BLOCK + x * ROWS, ROWS), ROWS)
    qo = []
    for j, dev in me.team():
        for src, dst in ((q_ref, qm_ref), (o_ref, om_ref)):
            qo.append(cp.make(
                src.at[:, pl.ds(pl.multiple_of(j * wide, wide), wide)], dst.at[rows, :], dev
            ))
    for i, (src, dst) in enumerate(((q_ref, qm_ref), (o_ref, om_ref))):
        own.append(pltpu.make_async_copy(
            src.at[:, pl.ds(pl.multiple_of(j_me * wide, wide), wide)], dst.at[rows, :],
            local.at[2 + i],
        ))
        own[-1].start()
    for copy in kvx:
        copy.wait_recv()
    own[0].wait()
    own[1].wait()

    first = (0, CUT)
    second = (CUT, BLOCK)

    def part(zz, yy, lohi, cc=c):
        lo, hi = lohi
        if yy is None:
            return kv_ref.at[zz, :, cc, :, pl.ds(lo, hi - lo), :]
        return kv_ref.at[zz, yy, cc, :, pl.ds(lo, hi - lo), :]

    def zz(d):
        return (z + d + NZ) % NZ

    def yy(d):
        return (y + d + NY) % NY

    def push(axis, step, zi, yi, lohi):
        ref = part(zi, yi, lohi)
        return cp.make(ref, ref, me.ring(axis, step))

    def y_send(zi, lohi):
        return push("y", 1, zi, y, lohi), push("y", -1, zi, y, lohi)

    def y_forward(zi, lohi, arrivals):
        a, b = halves(*lohi)
        arrivals[0].wait_recv()
        fa = push("y", 1, zi, yy(-1), a)
        arrivals[1].wait_recv()
        fb = push("y", -1, zi, yy(1), b)
        return fa, fb

    sib = []

    def to_sibling(zi, lohi):
        ref = part(zi, None, lohi)
        sib.append(cp.make(ref, ref, me.sibling()))

    def y_finish(zi, lohi, arrivals):
        arrivals[0].wait_recv()
        arrivals[1].wait_recv()
        if lohi is first:
            to_sibling(zi, lohi)

    z1 = push("z", 1, z, y, first), push("z", -1, z, y, first)
    y2 = y_send(z, second)
    stage = [(z, y_send(z, first))]
    y2 = y_forward(z, second, y2)
    y_finish(z, second, y2)
    z2 = push("z", 1, z, None, second), push("z", -1, z, None, second)
    to_sibling(z, second)
    forwarded = []
    for d in range(1, NZ // 2 + 1):
        new = []
        if d < NZ // 2:
            a, b = halves(*first) if d == NZ // 2 - 1 else (first, first)
            z1[0].wait_recv()
            up = push("z", 1, zz(-d), y, a)
            new.append((zz(-d), y_send(zz(-d), first)))
            z1[1].wait_recv()
            down = push("z", -1, zz(d), y, b)
            new.append((zz(d), y_send(zz(d), first)))
            z1 = up, down
        else:
            z1[0].wait_recv()
            z1[1].wait_recv()
            new.append((zz(d), y_send(zz(d), first)))
        done = forwarded
        forwarded = [(zi, y_forward(zi, first, arr)) for zi, arr in stage]
        stage = new
        if d < NZ // 2:
            a, b = halves(*second) if d == NZ // 2 - 1 else (second, second)
            z2[0].wait_recv()
            up = push("z", 1, zz(-d), None, a)
            to_sibling(zz(-d), second)
            z2[1].wait_recv()
            down = push("z", -1, zz(d), None, b)
            to_sibling(zz(d), second)
            z2 = up, down
        for zi, arr in done:
            y_finish(zi, first, arr)
    for zi, arr in forwarded:
        y_finish(zi, first, arr)
    forwarded = [(zi, y_forward(zi, first, arr)) for zi, arr in stage]
    z2[0].wait_recv()
    z2[1].wait_recv()
    to_sibling(zz(NZ // 2), second)
    for zi, arr in forwarded:
        y_finish(zi, first, arr)
    for copy in sib:
        copy.wait_recv()
    for copy in qo:
        copy.wait_recv()
    own[2].wait()
    own[3].wait()
    cp.finish()
    assert cp.count <= N_GATHER


def gather(q, o, k, v):
    wide = QHEADS * HEAD
    any_spec = pl.BlockSpec(memory_space=pl.ANY)
    return pl.pallas_call(
        gather_kernel,
        out_shape=[
            jax.ShapeDtypeStruct((SLOTS * SPAN, wide), BF16),
            jax.ShapeDtypeStruct((SLOTS * SPAN, wide), BF16),
            jax.ShapeDtypeStruct((NZ, NY, NC, 2, BLOCK, HEAD), BF16),
        ],
        in_specs=[any_spec] * 4,
        out_specs=[any_spec] * 3,
        scratch_shapes=[
            pltpu.SemaphoreType.DMA((N_GATHER,)),
            pltpu.SemaphoreType.DMA((N_GATHER,)),
            pltpu.SemaphoreType.DMA((4,)),
        ],
        compiler_params=pltpu.CompilerParams(collective_id=0, has_side_effects=True),
        name="gather",
    )(q, o, k, v)


def attend_kernel(slot_ref, len_ref, q_ref, o_ref, kv_ref, dq_ref, part_ref,
                  qs, os_, s_scr, dp_scr, dqt):
    rail = lax.axis_index("rail")
    chip = rail // NC

    def clear(i, _):
        part_ref[i] = jnp.zeros(part_ref.shape[1:], BF16)
        return 0

    lax.fori_loop(0, part_ref.shape[0], clear, 0)

    lane = lax.broadcasted_iota(jnp.int32, (1, LANES), 1) % SPAN
    sub = lax.broadcasted_iota(jnp.int32, (SPAN, 1), 0)

    def one_slot(s, _):
        def find(i, pos):
            return jnp.where(slot_ref[i] == chip * SLOTS + s, i, pos)

        span = lax.fori_loop(0, NZ * NY * NC * 2, find, 0)
        base = span * SPAN
        rows = pl.ds(pl.multiple_of(s * SPAN, SPAN), SPAN)
        for h in range(QHEADS):
            qs[h * SPAN:(h + 1) * SPAN, :] = q_ref[rows, h * HEAD:(h + 1) * HEAD]
            os_[h * SPAN:(h + 1) * SPAN, :] = o_ref[rows, h * HEAD:(h + 1) * HEAD]

        qpos = base + lane
        qstart = jnp.zeros((1, LANES), jnp.int32)
        start0 = 0
        end = 0
        for i in range(len_ref.shape[0]):
            end = end + len_ref[i]
            qstart = jnp.where(qpos >= end, end, qstart)
            start0 = jnp.where(base >= end, end, start0)
        tiles = span - start0 // SPAN + 1

        def key_slot(t):
            slot = slot_ref[span - t]
            return slot // 2, pl.ds(pl.multiple_of((slot % 2) * SPAN, SPAN), SPAN)

        def first(t, carry):
            m, l = carry
            r, half = key_slot(t)
            st = lax.dot_general(kv_ref[r, 0, half, :], qs[...], (((1,), (1,)), ((), ())),
                                 preferred_element_type=F32) * (SCALE * LOG2E)
            kpos = base - t * SPAN + sub
            st = jnp.where((kpos >= qstart) & (kpos <= qpos), st, NEG)
            s_scr[t] = st
            m_new = jnp.maximum(m, jnp.max(st, axis=0, keepdims=True))
            l = l * jnp.exp2(m - m_new) + jnp.sum(jnp.exp2(st - m_new), axis=0, keepdims=True)
            return m_new, l

        m, l = lax.fori_loop(0, tiles, first,
                             (jnp.full((1, LANES), NEG, F32), jnp.zeros((1, LANES), F32)))
        lse = m + jnp.log2(l)

        def second(t, rd):
            r, half = key_slot(t)
            p = jnp.exp2(s_scr[t] - lse)
            s_scr[t] = p
            dv = jnp.dot(p.astype(BF16), os_[...], preferred_element_type=F32)
            part_ref[r, 1, half, :] = (part_ref[r, 1, half, :].astype(F32) + dv).astype(BF16)
            dp = lax.dot_general(kv_ref[r, 1, half, :], os_[...], (((1,), (1,)), ((), ())),
                                 preferred_element_type=F32)
            dp_scr[t] = dp
            return rd + jnp.sum(p * dp, axis=0, keepdims=True)

        rd = lax.fori_loop(0, tiles, second, jnp.zeros((1, LANES), F32))
        dqt[...] = jnp.zeros_like(dqt)

        def third(t, _):
            r, half = key_slot(t)
            ds = (s_scr[t] * (dp_scr[t] - rd)).astype(BF16)
            dk = jnp.dot(ds, qs[...], preferred_element_type=F32) * SCALE
            part_ref[r, 0, half, :] = (part_ref[r, 0, half, :].astype(F32) + dk).astype(BF16)
            dqt[...] += lax.dot_general(kv_ref[r, 0, half, :], ds, (((0,), (0,)), ((), ())),
                                        preferred_element_type=F32)
            return 0

        lax.fori_loop(0, tiles, third, 0)
        for h in range(QHEADS):
            dq_ref[rows, h * HEAD:(h + 1) * HEAD] = (
                (dqt[:, h * SPAN:(h + 1) * SPAN] * SCALE).T.astype(BF16)
            )
        return 0

    lax.fori_loop(0, SLOTS, one_slot, 0)


def attend(span_slot, doc_lengths, qm, om, kv):
    rails = NZ * NY * NC
    kv = kv.reshape(rails, 2, BLOCK, HEAD)
    smem = pl.BlockSpec(memory_space=pltpu.SMEM)
    vmem = pl.BlockSpec(memory_space=pltpu.VMEM)
    dq, part = pl.pallas_call(
        attend_kernel,
        out_shape=[
            jax.ShapeDtypeStruct(qm.shape, BF16),
            jax.ShapeDtypeStruct(kv.shape, BF16),
        ],
        in_specs=[smem, smem, vmem, vmem, vmem],
        out_specs=[vmem, vmem],
        scratch_shapes=[
            pltpu.VMEM((LANES, HEAD), BF16),
            pltpu.VMEM((LANES, HEAD), BF16),
            pltpu.VMEM((TILES, SPAN, LANES), F32),
            pltpu.VMEM((TILES, SPAN, LANES), F32),
            pltpu.VMEM((HEAD, LANES), F32),
        ],
        compiler_params=pltpu.CompilerParams(vmem_limit_bytes=48 * 1024 * 1024),
        name="attend",
    )(span_slot, doc_lengths, qm, om, kv)
    return dq, part.reshape(NZ, NY, NC, 2, BLOCK, HEAD)


N_SCATTER = 96


def scatter_kernel(dqm_ref, part_ref, dq_ref, dk_ref, dv_ref, acc, sib, yh, yf, z1h, z1f, z2h, z2f,
                   send, recv, local):
    me = Place()
    cp = Copies(send, recv)
    greet(me)
    x, z, y, c = me.x, me.z, me.y, me.c
    j_me = x * NC + c
    wide = QHEADS * HEAD
    D = NZ // 2
    first = (0, CUT)
    second = (CUT, BLOCK)

    def zz(d):
        return (z + d + NZ) % NZ

    def yy(d):
        return (y + d + NY) % NY

    order = [D]
    for d in range(D - 1, 0, -1):
        order += [d, -d]
    order.append(0)
    sibs, owns = {}, {}
    for i, d in enumerate(order):
        sibs[d] = cp.make(part_ref.at[zz(d), :, 1 - c], sib.at[zz(d)], me.sibling())
        owns[d] = pltpu.make_async_copy(part_ref.at[zz(d), :, c], acc.at[zz(d)], local.at[i])
        owns[d].start()
    dqs = []
    for j, dev in me.team():
        dqs.append(cp.make(
            dqm_ref.at[pl.ds(pl.multiple_of((j % NC) * BLOCK + (j // NC) * ROWS, ROWS), ROWS), :],
            dq_ref.at[:, pl.ds(pl.multiple_of(j_me * wide, wide), wide)], dev,
        ))
    dq_own = pltpu.make_async_copy(
        dqm_ref.at[pl.ds(pl.multiple_of(c * BLOCK + x * ROWS, ROWS), ROWS), :],
        dq_ref.at[:, pl.ds(pl.multiple_of(j_me * wide, wide), wide)], local.at[NZ],
    )
    dq_own.start()

    def slab(zi, yi, lohi):
        lo, hi = lohi
        if yi is None:
            return acc.at[zi, :, :, pl.ds(lo, hi - lo), :]
        return acc.at[zi, yi, :, pl.ds(lo, hi - lo), :]

    def add(dst, *srcs):
        total = dst[...].astype(F32)
        for src in srcs:
            total = total + src[...].astype(F32)
        dst[...] = total.astype(BF16)

    def add_planes(zi, lohi, src):
        def body(yi, _):
            add(slab(zi, yi, lohi), src.at[yi])
            return 0
        lax.fori_loop(0, NY, body, 0)

    fa, fb = halves(*first)
    sa, sb = halves(*second)

    def rows_of(ref, lohi):
        return ref.at[:, pl.ds(0, lohi[1] - lohi[0]), :]

    def y1(slot, zi, lohi, ab):
        a, b = ab
        return (
            cp.make(slab(zi, yy(2), a), rows_of(yh.at[slot, 0], a), me.ring("y", 1)),
            cp.make(slab(zi, yy(2), b), rows_of(yh.at[slot, 1], b), me.ring("y", -1)),
        )

    def y2(slot, zi, lohi, ab, arr):
        a, b = ab
        arr[0].wait_recv()
        add(slab(zi, yy(1), a), rows_of(yh.at[slot, 0], a))
        up = cp.make(slab(zi, yy(1), lohi), rows_of(yf.at[slot, 0], lohi), me.ring("y", 1))
        arr[1].wait_recv()
        add(slab(zi, yy(-1), b), rows_of(yh.at[slot, 1], b))
        down = cp.make(slab(zi, yy(-1), lohi), rows_of(yf.at[slot, 1], lohi), me.ring("y", -1))
        return up, down

    def y3(slot, zi, lohi, arr):
        arr[0].wait_recv()
        arr[1].wait_recv()
        add(slab(zi, y, lohi), rows_of(yf.at[slot, 0], lohi), rows_of(yf.at[slot, 1], lohi))

    yarr = {}

    def stage0(i):
        d = order[i]
        owns[d].wait()
        sibs[d].wait_recv()
        add_planes(zz(d), (0, BLOCK), sib.at[zz(d)])
        yarr[d] = y1(i, zz(d), first, (fa, fb))

    def ystep2(i):
        d = order[i]
        yarr[d] = y2(i, zz(d), first, (fa, fb), yarr[d])

    def ystep3(i):
        d = order[i]
        y3(i, zz(d), first, yarr[d])

    def z1_half():
        return (
            cp.make(slab(zz(D), y, fa), rows_of(z1h.at[0], fa), me.ring("z", 1)),
            cp.make(slab(zz(D), y, fb), rows_of(z1h.at[1], fb), me.ring("z", -1)),
        )

    def z2_half():
        return (
            cp.make(slab(zz(D), None, sa), z2h.at[0, :, :, pl.ds(0, sa[1] - sa[0]), :], me.ring("z", 1)),
            cp.make(slab(zz(D), None, sb), z2h.at[1, :, :, pl.ds(0, sb[1] - sb[0]), :], me.ring("z", -1)),
        )

    def z1_step(d, arr):
        a, b = (fa, fb) if d == D - 1 else (first, first)
        src = z1h if d == D - 1 else z1f.at[d]
        arr[0].wait_recv()
        add(slab(zz(d), y, a), rows_of(src.at[0], a))
        up = cp.make(slab(zz(d), y, first), z1f.at[d - 1, 0], me.ring("z", 1))
        arr[1].wait_recv()
        add(slab(zz(-d), y, b), rows_of(src.at[1], b))
        down = cp.make(slab(zz(-d), y, first), z1f.at[d - 1, 1], me.ring("z", -1))
        return up, down

    def z2_step(d, arr):
        a, b = (sa, sb) if d == D - 1 else (second, second)
        src = z2h if d == D - 1 else z2f.at[d]
        arr[0].wait_recv()
        add_planes(zz(d), a, src.at[0, :, :, pl.ds(0, a[1] - a[0]), :])
        up = cp.make(slab(zz(d), None, second), z2f.at[d - 1, 0], me.ring("z", 1))
        arr[1].wait_recv()
        add_planes(zz(-d), b, src.at[1, :, :, pl.ds(0, b[1] - b[0]), :])
        down = cp.make(slab(zz(-d), None, second), z2f.at[d - 1, 1], me.ring("z", -1))
        return up, down

    stage0(0)
    z2 = z2_half()
    stage0(1)
    stage0(2)
    ystep2(0)
    z2 = z2_step(3, z2)
    stage0(3)
    stage0(4)
    ystep3(0)
    z1 = z1_half()
    ystep2(1)
    ystep2(2)
    z2 = z2_step(2, z2)
    stage0(5)
    stage0(6)
    stage0(7)
    ystep3(1)
    ystep3(2)
    z1 = z1_step(3, z1)
    ystep2(3)
    ystep2(4)
    z2 = z2_step(1, z2)
    ystep3(3)
    ystep3(4)
    z1 = z1_step(2, z1)
    ystep2(5)
    ystep2(6)
    ystep2(7)
    z2[0].wait_recv()
    z2[1].wait_recv()
    add_planes(z, second, z2f.at[0, 0])
    add_planes(z, second, z2f.at[0, 1])
    last = y1(NZ, z, second, (sa, sb))
    ystep3(5)
    ystep3(6)
    z1 = z1_step(1, z1)
    last = y2(NZ, z, second, (sa, sb), last)
    ystep3(7)
    y3(NZ, z, second, last)
    z1[0].wait_recv()
    z1[1].wait_recv()
    add(slab(z, y, first), z1f.at[0, 0], z1f.at[0, 1])

    back = []
    mine = pl.ds(pl.multiple_of(x * HEAD, HEAD), HEAD)
    for step in range(1, NX):
        to = (x + step) % NX
        for i, ref in enumerate((dk_ref, dv_ref)):
            back.append(cp.make(
                acc.at[z, y, i, pl.ds(pl.multiple_of(to * ROWS, ROWS), ROWS), :],
                ref.at[:, mine], me.at(x=to),
            ))
    own = []
    for i, ref in enumerate((dk_ref, dv_ref)):
        own.append(pltpu.make_async_copy(
            acc.at[z, y, i, pl.ds(pl.multiple_of(x * ROWS, ROWS), ROWS), :],
            ref.at[:, mine], local.at[NZ + 1 + i],
        ))
        own[-1].start()
    for copy in dqs + back:
        copy.wait_recv()
    dq_own.wait()
    for copy in own:
        copy.wait()
    cp.finish()
    assert cp.count <= N_SCATTER


def scatter(dqm, part):
    any_spec = pl.BlockSpec(memory_space=pl.ANY)
    rest = BLOCK - CUT
    half = max(h[1] - h[0] for h in halves(0, CUT))
    rest_half = max(h[1] - h[0] for h in halves(CUT, BLOCK))
    D = NZ // 2
    return pl.pallas_call(
        scatter_kernel,
        out_shape=[
            jax.ShapeDtypeStruct((ROWS, NX * NC * QHEADS * HEAD), BF16),
            jax.ShapeDtypeStruct((ROWS, NX * HEAD), BF16),
            jax.ShapeDtypeStruct((ROWS, NX * HEAD), BF16),
        ],
        in_specs=[any_spec] * 2,
        out_specs=[any_spec] * 3,
        scratch_shapes=[
            pltpu.VMEM((NZ, NY, 2, BLOCK, HEAD), BF16),
            pltpu.VMEM((NZ, NY, 2, BLOCK, HEAD), BF16),
            pltpu.VMEM((NZ + 1, 2, 2, half, HEAD), BF16),
            pltpu.VMEM((NZ + 1, 2, 2, CUT, HEAD), BF16),
            pltpu.VMEM((2, 2, half, HEAD), BF16),
            pltpu.VMEM((D - 1, 2, 2, CUT, HEAD), BF16),
            pltpu.VMEM((2, NY, 2, rest_half, HEAD), BF16),
            pltpu.VMEM((D - 1, 2, NY, 2, rest, HEAD), BF16),
            pltpu.SemaphoreType.DMA((N_SCATTER,)),
            pltpu.SemaphoreType.DMA((N_SCATTER,)),
            pltpu.SemaphoreType.DMA((NZ + 3,)),
        ],
        compiler_params=pltpu.CompilerParams(
            collective_id=1, has_side_effects=True, vmem_limit_bytes=48 * 1024 * 1024
        ),
        name="scatter",
    )(dqm, part)


def per_device(queries, keys, values, output_cotangent, doc_lengths, span_slot):
    qm, om, kv = gather(queries, output_cotangent, keys, values)
    dqm, part = attend(span_slot, doc_lengths, qm, om, kv)
    return tuple(scatter(dqm, part))


def solution(mesh):
    rows = P(("rail", "node"), None)
    return jax.shard_map(
        per_device, mesh=mesh, in_specs=(rows, rows, rows, rows, P(), P()),
        out_specs=(rows, rows, rows), check_vma=False,
    )
```

```python
import math

import jax
import jax.numpy as jnp
from jax import lax
from jax.experimental import pallas as pl
from jax.experimental.pallas import tpu as pltpu
from jax.sharding import PartitionSpec as P

HEAD = 128
SPAN = 128
NX, NZ, NY, NC = 4, 8, 4, 2
ROWS = 64
BLOCK = NX * ROWS
SLOTS = 4
NSLOT = NZ * NY * SLOTS
QHEADS = 4
LANES = QHEADS * SPAN
WIDE = QHEADS * HEAD
STEP = 256
STEPS = 9
WIN = STEP * STEPS
WT = WIN // SPAN
HALF = SPAN // 2
FAR = NZ // 2
SCALE = 1.0 / math.sqrt(HEAD)
C2 = SCALE * 1.4426950408889634
NEG = -1e30
MESH = pl.DeviceIdType.MESH
F32 = jnp.float32
BF16 = jnp.bfloat16
N_SEM = 320
COLUMNS = [0, 1, -1, 2, -2, 3, -3, 4]


class Place:
    def __init__(self):
        self.x = lax.axis_index("node")
        rail = lax.axis_index("rail")
        self.c = rail % NC
        self.y = (rail // NC) % NY
        self.z = rail // (NC * NY)

    def at(self, x=None, z=None, y=None, c=None):
        x = self.x if x is None else x
        z = self.z if z is None else z
        y = self.y if y is None else y
        c = self.c if c is None else c
        return (x, (z * NY + y) * NC + c)

    def zz(self, d):
        return (self.z + d + NZ) % NZ

    def yy(self, d):
        return (self.y + d + NY) % NY

    def ring(self, axis, step):
        return self.at(z=self.zz(step)) if axis == "z" else self.at(y=self.yy(step))

    def sibling(self):
        return self.at(c=1 - self.c)

    def team(self):
        out = []
        for step in range(1, NX * NC):
            j = (self.x * NC + self.c + step) % (NX * NC)
            out.append((j, self.at(x=j // NC, c=j % NC)))
        return out


def greet(place):
    barrier = pltpu.get_barrier_semaphore()
    peers = [dev for _, dev in place.team()]
    peers += [place.ring("z", 1), place.ring("z", -1)]
    peers += [place.ring("y", k) for k in range(1, NY)]
    for dev in peers:
        pl.semaphore_signal(barrier, inc=1, device_id=dev, device_id_type=MESH)
    pl.semaphore_wait(barrier, len(peers))


class Copies:
    def __init__(self, send, recv):
        self.send, self.recv, self.count = send, recv, 0

    def make(self, src, dst, dev):
        i = self.count
        self.count += 1
        return pltpu.make_async_remote_copy(
            src_ref=src, dst_ref=dst, send_sem=self.send.at[i], recv_sem=self.recv.at[i],
            device_id=dev, device_id_type=MESH,
        )


def line(z, c, b):
    return ((z * NC + c) * 2 + b) * NY


class Gather:
    def __init__(self, me, cp, ref):
        self.ref = ref
        c, y = me.c, me.y

        def blk(zi, yi, b, lo=0, n=SPAN):
            return ref.at[line(zi, c, b) + yi, pl.ds(lo, n), :]

        self.z = [{}, {}]
        self.z2 = [[{} for _ in range(NY)] for _ in range(2)]
        for d in range(1, FAR + 1):
            for i, sign in enumerate((1, -1)):
                lo, n = (i * HALF, HALF) if d == FAR else (0, SPAN)
                zi = me.zz(-sign * (d - 1))
                to = me.ring("z", sign)
                src = blk(zi, y, 0, lo, n)
                self.z[i][d] = cp.make(src, src, to)
                for k in range(NY):
                    src = blk(zi, me.yy(k), 1, lo, n)
                    self.z2[i][k][d] = cp.make(src, src, to)
        self.y = {}
        for d in COLUMNS:
            src = blk(me.zz(d), y, 0)
            self.y[d] = [cp.make(src, src, me.ring("y", k)) for k in range(1, NY)]
        src = blk(me.z, y, 1)
        self.y2 = [cp.make(src, src, me.ring("y", k)) for k in range(1, NY)]
        self.sib = [{}, {}]
        for d in COLUMNS:
            for b in range(2):
                src = ref.at[pl.ds(line(me.zz(d), c, b), NY)]
                self.sib[b][d] = cp.make(src, src, me.sibling())

    def begin(self):
        for copy in self.y2:
            copy.start()
        for i in range(2):
            self.z[i][1].start()
        for i in range(2):
            self.z2[i][0][1].start()
        for copy in self.y[0]:
            copy.start()

    def second(self):
        for k in range(1, NY):
            self.y2[k - 1].wait_recv()
            for i in range(2):
                self.z2[i][NY - k][1].start()
        self.sib[1][0].start()

    def zstep(self, d):
        for i, sign in enumerate((1, -1)):
            self.z[i][d].wait_recv()
            if d < FAR:
                self.z[i][d + 1].start()
                for copy in self.y[-sign * d]:
                    copy.start()
        if d == FAR:
            for copy in self.y[FAR]:
                copy.start()
        for k in (0, 3, 2, 1):
            for i in range(2):
                self.z2[i][k][d].wait_recv()
                if d < FAR:
                    self.z2[i][k][d + 1].start()
        self.sib[1][d].start()
        if d < FAR:
            self.sib[1][-d].start()

    def finish(self, *cols):
        for d in cols:
            for copy in self.y[d]:
                copy.wait_recv()
            self.sib[0][d].start()

    def done(self):
        for b in (1, 0):
            for d in COLUMNS:
                self.sib[b][d].wait_recv()

    def drain(self):
        for i in range(2):
            for d in range(1, FAR + 1):
                self.z[i][d].wait_send()
                for k in range(NY):
                    self.z2[i][k][d].wait_send()
        for d in COLUMNS:
            for copy in self.y[d]:
                copy.wait_send()
            for b in range(2):
                self.sib[b][d].wait_send()
        for copy in self.y2:
            copy.wait_send()


def add(dst, *srcs):
    total = dst[...].astype(F32)
    for src in srcs:
        total = total + src[...].astype(F32)
    dst[...] = total.astype(BF16)


class Scatter:
    def __init__(self, me, cp, window, source, bufs):
        self.me, self.window, self.source = me, window, source
        (self.acc, self.snd, self.sibr, self.yr, self.yr1,
         self.zr0h, self.zr0f, self.zr1h, self.zr1f) = bufs
        acc, y = self.acc, me.y
        self.sib, self.y0 = {}, {}
        for i, d in enumerate(COLUMNS):
            self.sib[d] = cp.make(self.snd.at[me.zz(d)], self.sibr.at[me.zz(d)], me.sibling())
            self.y0[d] = [
                cp.make(acc.at[me.zz(d), me.yy(k), 0], self.yr.at[i, k - 1], me.ring("y", k))
                for k in range(1, NY)
            ]
        self.y1 = [cp.make(acc.at[me.z, me.yy(k), 1], self.yr1.at[k - 1], me.ring("y", k))
                   for k in range(1, NY)]
        self.z0 = [{}, {}]
        self.z1 = [[{}, {}], [{}, {}]]
        for d in range(FAR, 0, -1):
            for i, sign in enumerate((1, -1)):
                to = me.ring("z", sign)
                zi = me.zz(sign * d)
                rows = pl.ds(i * HALF, HALF) if d == FAR else pl.ds(0, SPAN)
                dst = self.zr0h.at[i] if d == FAR else self.zr0f.at[d - 1, i]
                self.z0[i][d] = cp.make(acc.at[zi, y, 0, rows, :], dst, to)
                for h in range(2):
                    ys = pl.ds(2 * h, 2)
                    dst = self.zr1h.at[i, ys] if d == FAR else self.zr1f.at[d - 1, i, ys]
                    self.z1[i][h][d] = cp.make(acc.at[zi, ys, 1, rows, :], dst, to)

    def drain(self):
        for d in COLUMNS:
            self.sib[d].wait_send()
            for copy in self.y0[d]:
                copy.wait_send()
        for copy in self.y1:
            copy.wait_send()
        for i in range(2):
            for d in range(1, FAR + 1):
                self.z0[i][d].wait_send()
                for h in range(2):
                    self.z1[i][h][d].wait_send()

    def collect(self, d):
        me = self.me
        zi = me.zz(d)

        def tiles(core, dst):
            def body(i, _):
                yi, b = i // 2, i % 2
                j = line(zi, core, b) + yi
                total = None
                for s in range(SLOTS):
                    w = self.source[s * NSLOT + j]
                    tile = self.window[w]
                    total = tile if total is None else total + tile
                dst[zi, yi, b] = total
                return 0
            lax.fori_loop(0, NY * 2, body, 0, unroll=4)

        tiles(1 - me.c, self.snd)
        self.sib[d].start()
        tiles(me.c, self.acc)

    def pair(self, *cols):
        me = self.me
        for d in cols:
            zi = me.zz(d)
            self.sib[d].wait_recv()

            def body(yi, _):
                add(self.acc.at[zi, yi], self.sibr.at[zi, yi])
                return 0

            lax.fori_loop(0, NY, body, 0)
            for copy in self.y0[d]:
                copy.start()
            if d == FAR:
                for h in range(2):
                    for i in range(2):
                        self.z1[i][h][d].start()

    def yadd(self, *cols):
        me = self.me
        for d in cols:
            j = COLUMNS.index(d)
            for copy in self.y0[d]:
                copy.wait_recv()
            add(self.acc.at[me.zz(d), me.y, 0], *[self.yr.at[j, k] for k in range(NY - 1)])
            if d == FAR:
                for i in range(2):
                    self.z0[i][d].start()

    def z0step(self, d):
        me = self.me
        for i, sign in enumerate((1, -1)):
            self.z0[i][d + 1].wait_recv()
            zi = me.zz(sign * d)
            if d == FAR - 1:
                add(self.acc.at[zi, me.y, 0, pl.ds(i * HALF, HALF), :], self.zr0h.at[i])
            else:
                add(self.acc.at[zi, me.y, 0], self.zr0f.at[d, i])
            self.z0[i][d].start()

    def z1step(self, d):
        me = self.me
        for h in range(2):
            for i, sign in enumerate((1, -1)):
                self.z1[i][h][d + 1].wait_recv()
                zi = me.zz(sign * d)
                for yi in range(2 * h, 2 * h + 2):
                    if d == FAR - 1:
                        add(self.acc.at[zi, yi, 1, pl.ds(i * HALF, HALF), :], self.zr1h.at[i, yi])
                    else:
                        add(self.acc.at[zi, yi, 1], self.zr1f.at[d, i, yi])
                self.z1[i][h][d].start()

    def z1last(self):
        me = self.me
        for h in range(2):
            for i in range(2):
                self.z1[i][h][1].wait_recv()
            for yi in range(2 * h, 2 * h + 2):
                add(self.acc.at[me.z, yi, 1], self.zr1f.at[0, 0, yi], self.zr1f.at[0, 1, yi])
        for copy in self.y1:
            copy.start()

    def z0last(self):
        me = self.me
        for i in range(2):
            self.z0[i][1].wait_recv()
        add(self.acc.at[me.z, me.y, 0], self.zr0f.at[0, 0], self.zr0f.at[0, 1])

    def y1last(self):
        me = self.me
        for copy in self.y1:
            copy.wait_recv()
        add(self.acc.at[me.z, me.y, 1], *[self.yr1.at[k] for k in range(NY - 1)])


def fold(x, op):
    return op(x.reshape(x.shape[0] // 8, 8, x.shape[1]), axis=0)


def at_step(t):
    return pl.ds(t * STEP, STEP)


def span_rows(i):
    return pl.ds(pl.multiple_of(i * SPAN, SPAN), SPAN)


def load_window(s, seen, src, put):
    def body(w, _):
        j = seen[s * WT + w]
        put(w, src[j])
        return 0

    lax.fori_loop(0, WT, body, 0, unroll=2)


def tables_kernel(slot_ref, len_ref, seen, source, rows_ref, span_of):
    chip = lax.axis_index("rail") // NC
    lane = lax.broadcasted_iota(jnp.int32, (1, LANES), 1) % SPAN

    def invert(i, _):
        span_of[slot_ref[i]] = i
        return 0

    lax.fori_loop(0, NSLOT, invert, 0, unroll=8)

    for s in range(SLOTS):
        def clear(i, _):
            source[s * NSLOT + i] = s * WT
            return 0

        lax.fori_loop(0, NSLOT, clear, 0, unroll=8)
        span = span_of[chip * SLOTS + s]
        seen[s * WT] = 0

        def fill(w, _):
            n = span - (WT - 1) + w
            j = slot_ref[jnp.maximum(n, 0)]
            j = (j // 16) * 16 + (j % 4) * 4 + (j // 4) % 4
            seen[s * WT + w] = j

            @pl.when(n >= 0)
            def _():
                source[s * NSLOT + j] = s * WT + w

            return 0

        lax.fori_loop(1, WT, fill, 0)
        qpos = span * SPAN + lane
        qstart = jnp.zeros((1, LANES), jnp.int32)
        end = 0
        for i in range(len_ref.shape[0]):
            end = end + len_ref[i]
            qstart = jnp.where(qpos >= end, end, qstart)
        rows_ref[s, 0:1, :] = qstart - (span - (WT - 1)) * SPAN
        rows_ref[s, 1:2, :] = qpos - qstart


def kernel(seen, source, rows_ref, q_ref, o_ref, k_ref, v_ref, dq_ref, dk_ref, dv_ref,
           k_all, v_all, qm, om, kw, vw, qs, os_, tq, s_scr, p_scr, wk, wv, inv_scr, dqt, dqm,
           *rest):
    bufs_v, bufs_k = rest[:9], rest[9:18]
    send, recv, local = rest[18:]
    me = Place()
    cp = Copies(send, recv)
    x, z, y, c = me.x, me.z, me.y, me.c
    j_me = x * NC + c

    def cols(j, n):
        return pl.ds(pl.multiple_of(j * n, n), n)

    kvx = [[], []]
    own = []
    mine = pl.ds(pl.multiple_of((x % 2) * ROWS, ROWS), ROWS)
    for i, (src, dst) in enumerate(((k_ref, k_all), (v_ref, v_all))):
        for step in range(1, NX):
            to = (x + step) % NX
            kvx[i].append(cp.make(
                src.at[:, cols(to, HEAD)], dst.at[line(z, c, x // 2) + y, mine, :], me.at(x=to)))
        own.append(pltpu.make_async_copy(
            src.at[:, cols(x, HEAD)], dst.at[line(z, c, x // 2) + y, mine, :], local.at[i]))
    rows = pl.ds(pl.multiple_of(c * BLOCK + x * ROWS, ROWS), ROWS)
    qo = []
    for j, dev in me.team():
        for src, dst in ((q_ref, qm), (o_ref, om)):
            qo.append(cp.make(src.at[:, cols(j, WIDE)], dst.at[rows, :], dev))
    for i, (src, dst) in enumerate(((q_ref, qm), (o_ref, om))):
        own.append(pltpu.make_async_copy(
            src.at[:, cols(j_me, WIDE)], dst.at[rows, :], local.at[2 + i]))
    gk, gv = Gather(me, cp, k_all), Gather(me, cp, v_all)
    sv = Scatter(me, cp, wv, source, bufs_v)
    sk = Scatter(me, cp, wk, source, bufs_k)
    dqs = []
    for j, dev in me.team():
        there = pl.ds(pl.multiple_of((j % NC) * BLOCK + (j // NC) * ROWS, ROWS), ROWS)
        dqs.append(cp.make(dqm.at[there, :], dq_ref.at[:, cols(j_me, WIDE)], dev))
    own.append(pltpu.make_async_copy(dqm.at[rows, :], dq_ref.at[:, cols(j_me, WIDE)], local.at[4]))
    back = [[], []]
    for i, (acc, dst) in enumerate(((bufs_k[0], dk_ref), (bufs_v[0], dv_ref))):
        for step in range(1, NX):
            to = (x + step) % NX
            part = pl.ds(pl.multiple_of((to % 2) * ROWS, ROWS), ROWS)
            back[i].append(cp.make(
                acc.at[z, y, to // 2, part, :], dst.at[:, cols(x, HEAD)], me.at(x=to)))
        own.append(pltpu.make_async_copy(
            acc.at[z, y, x // 2, mine, :], dst.at[:, cols(x, HEAD)], local.at[5 + i]))
    assert cp.count <= N_SEM

    greet(me)
    for i in range(2):
        for copy in kvx[i]:
            copy.start()
        own[i].start()
    for copy in qo:
        copy.start()
    own[2].start()
    own[3].start()

    for copy in kvx[0]:
        copy.wait_recv()
    own[0].wait()
    gk.begin()
    gk.second()
    for copy in kvx[1]:
        copy.wait_recv()
    own[1].wait()
    gv.begin()
    gk.zstep(1)
    gk.finish(0)
    gv.second()
    gk.zstep(2)
    gk.finish(1, -1)
    gk.zstep(3)
    gv.zstep(1)
    gk.finish(2, -2)
    gk.zstep(4)
    gk.finish(3, -3)
    gv.finish(0)
    gv.zstep(2)
    gk.finish(4)
    gk.done()
    for copy in qo:
        copy.wait_recv()
    own[2].wait()
    own[3].wait()

    sub = lax.broadcasted_iota(jnp.int32, (STEP, 1), 0)

    def during(s, table):
        for i, events in enumerate(table):
            if events:
                @pl.when(s == i)
                def _():
                    for event in events:
                        event()

    def first_part(s, _):
        low, extra = rows_ref[s, 0:1, :], rows_ref[s, 1:2, :]

        def put(w, tile):
            kw[s, span_rows(w), :] = tile

        load_window(s, seen, k_all, put)
        for h in range(QHEADS):
            qh = qm[span_rows(s), h * HEAD:(h + 1) * HEAD]
            qs[s, h * SPAN:(h + 1) * SPAN, :] = qh
            tq[:, h * SPAN:(h + 1) * SPAN] = qh.T
        top = jnp.full((8, LANES), NEG, F32)
        for t in range(STEPS):
            st = jnp.dot(kw[s, at_step(t), :], tq[...], preferred_element_type=F32)
            rel = (sub + t * STEP) - low
            st = jnp.where((rel >= 0) & (rel <= extra), st, NEG)
            s_scr[t] = st
            top = jnp.maximum(top, fold(st, jnp.max))
        during(s, v_events[0])
        mc = jnp.max(top, axis=0, keepdims=True) * C2
        total = jnp.zeros((8, LANES), F32)
        for t in range(STEPS):
            p = jnp.exp2(s_scr[t] * C2 - mc)
            p_scr[s, t] = p.astype(BF16)
            total = total + fold(p, jnp.sum)
        inv = 1.0 / jnp.sum(total, axis=0, keepdims=True)
        inv8 = jnp.broadcast_to(inv, (8, LANES))
        inv_scr[s] = inv8
        for h in range(QHEADS):
            col = inv8[:, h * SPAN:(h + 1) * SPAN].T[:, :1]
            oh = om[span_rows(s), h * HEAD:(h + 1) * HEAD].astype(F32)
            os_[s, h * SPAN:(h + 1) * SPAN, :] = (oh * col).astype(BF16)
        during(s, v_events[1])
        for t in range(STEPS):
            dv = jnp.dot(p_scr[s, t], os_[s], preferred_element_type=F32)
            wv[pl.ds(s * WT + 2 * t, 2)] = dv.astype(BF16).reshape(2, SPAN, HEAD)
        during(s, v_events[2])
        return 0

    v_events = [
        [[lambda: gv.finish(1, -1)], [lambda: gv.zstep(4)], [lambda: gv.finish(3, -3)], None],
        [None, None, None, None],
        [[lambda: gv.zstep(3)], [lambda: gv.finish(2, -2)], [lambda: gv.finish(4)], None],
    ]
    lax.fori_loop(0, SLOTS, first_part, 0)
    gv.done()

    sv.collect(4)
    sv.collect(3)
    sv.collect(-3)
    sv.pair(4)
    sv.pair(3, -3)

    def second_part(s, _):

        def put(w, tile):
            vw[span_rows(w), :] = tile

        load_window(s, seen, v_all, put)
        for h in range(QHEADS):
            tq[:, h * SPAN:(h + 1) * SPAN] = os_[s, h * SPAN:(h + 1) * SPAN, :].T
        total = jnp.zeros((8, LANES), F32)
        for t in range(STEPS):
            dp = jnp.dot(vw[at_step(t), :], tq[...], preferred_element_type=F32)
            s_scr[t] = dp
            total = total + fold(p_scr[s, t].astype(F32) * dp, jnp.sum)
        during(s, k_events[0])
        dots = jnp.sum(total, axis=0, keepdims=True) * inv_scr[s, :1, :]
        dqt[...] = jnp.zeros_like(dqt)
        for t in range(STEPS):
            ds = (p_scr[s, t].astype(F32) * (s_scr[t] - dots)).astype(BF16)
            dk = jnp.dot(ds, qs[s], preferred_element_type=F32) * SCALE
            wk[pl.ds(s * WT + 2 * t, 2)] = dk.astype(BF16).reshape(2, SPAN, HEAD)
            dqt[...] += lax.dot_general(kw[s, at_step(t), :], ds, (((0,), (0,)), ((), ())),
                                        preferred_element_type=F32)
        for h in range(QHEADS):
            dqm[span_rows(s), h * HEAD:(h + 1) * HEAD] = (
                (dqt[:, h * SPAN:(h + 1) * SPAN] * SCALE).T.astype(BF16))
        during(s, k_events[1])
        return 0

    k_events = [
        [
            [lambda: sv.collect(2), lambda: sv.collect(-2)],
            [lambda: sv.collect(1), lambda: sv.collect(-1), lambda: sv.z1step(2)],
            [lambda: sv.collect(0), lambda: sv.pair(1, -1)],
            [lambda: sv.z0step(2), lambda: sv.z1step(1)],
        ],
        [
            [lambda: sv.z1step(3), lambda: sv.pair(2, -2), lambda: sv.yadd(4)],
            [lambda: sv.yadd(3, -3), lambda: sv.z0step(3)],
            [lambda: sv.yadd(2, -2), lambda: sv.pair(0)],
            [lambda: sv.yadd(1, -1)],
        ],
    ]
    lax.fori_loop(0, SLOTS, second_part, 0)
    for copy in dqs:
        copy.start()
    own[4].start()

    sk.collect(4)
    sv.z0step(1)
    sk.collect(3)
    sk.collect(-3)
    sk.pair(4)
    sv.z1last()
    sk.collect(2)
    sk.collect(-2)
    sk.pair(3, -3)
    sv.yadd(0)
    sk.yadd(4)
    sk.collect(1)
    sk.collect(-1)
    sk.z1step(3)
    sk.pair(2, -2)
    sv.z0last()
    sk.yadd(3, -3)
    sk.z0step(3)
    sk.collect(0)
    sv.y1last()
    for copy in back[1]:
        copy.start()
    own[6].start()
    sk.pair(1, -1)
    sk.pair(0)
    sk.z1step(2)
    sk.yadd(2, -2)
    sk.z0step(2)
    sk.yadd(1, -1)
    gk.drain()
    sk.z1step(1)
    sk.z0step(1)
    sk.yadd(0)
    gv.drain()
    sk.z1last()
    for copy in kvx[0] + kvx[1] + qo:
        copy.wait_send()
    sk.z0last()
    sv.drain()
    sk.y1last()
    for copy in back[0]:
        copy.start()
    own[5].start()
    sk.drain()
    for copy in dqs + back[1] + back[0]:
        copy.wait_recv()
        copy.wait_send()
    for i in (4, 5, 6):
        own[i].wait()


def per_device(queries, keys, values, output_cotangent, doc_lengths, span_slot):
    smem = pl.BlockSpec(memory_space=pltpu.SMEM)
    any_spec = pl.BlockSpec(memory_space=pl.ANY)

    def vmem(*shape, dtype=BF16):
        return pltpu.VMEM(shape, dtype)

    scatter_bufs = [
        vmem(NZ, NY, 2, SPAN, HEAD),
        vmem(NZ, NY, 2, SPAN, HEAD),
        vmem(NZ, NY, 2, SPAN, HEAD),
        vmem(NZ, NY - 1, SPAN, HEAD),
        vmem(NY - 1, SPAN, HEAD),
        vmem(2, HALF, HEAD),
        vmem(FAR - 1, 2, SPAN, HEAD),
        vmem(2, NY, HALF, HEAD),
        vmem(FAR - 1, 2, NY, SPAN, HEAD),
    ]
    seen, source, rows = pl.pallas_call(
        tables_kernel,
        out_shape=[
            jax.ShapeDtypeStruct((SLOTS * WT,), jnp.int32),
            jax.ShapeDtypeStruct((SLOTS * NSLOT,), jnp.int32),
            jax.ShapeDtypeStruct((SLOTS, 8, LANES), jnp.int32),
        ],
        in_specs=[smem] * 2,
        out_specs=[smem, smem, pl.BlockSpec(memory_space=pltpu.VMEM)],
        scratch_shapes=[pltpu.SMEM((NSLOT,), jnp.int32)],
        name="tables",
    )(span_slot, doc_lengths)
    outs = pl.pallas_call(
        kernel,
        out_shape=[
            jax.ShapeDtypeStruct(queries.shape, BF16),
            jax.ShapeDtypeStruct(keys.shape, BF16),
            jax.ShapeDtypeStruct(values.shape, BF16),
        ],
        in_specs=[smem] * 2 + [pl.BlockSpec(memory_space=pltpu.VMEM)] + [any_spec] * 4,
        out_specs=[any_spec] * 3,
        scratch_shapes=[
            vmem(NSLOT, SPAN, HEAD),
            vmem(NSLOT, SPAN, HEAD),
            vmem(SLOTS * SPAN, WIDE),
            vmem(SLOTS * SPAN, WIDE),
            vmem(SLOTS, WIN, HEAD),
            vmem(WIN, HEAD),
            vmem(SLOTS, LANES, HEAD),
            vmem(SLOTS, LANES, HEAD),
            vmem(HEAD, LANES),
            vmem(STEPS, STEP, LANES, dtype=F32),
            vmem(SLOTS, STEPS, STEP, LANES),
            vmem(SLOTS * WT, SPAN, HEAD),
            vmem(SLOTS * WT, SPAN, HEAD),
            vmem(SLOTS, 8, LANES, dtype=F32),
            vmem(HEAD, LANES, dtype=F32),
            vmem(SLOTS * SPAN, WIDE),
        ] + scatter_bufs * 2 + [
            pltpu.SemaphoreType.DMA((N_SEM,)),
            pltpu.SemaphoreType.DMA((N_SEM,)),
            pltpu.SemaphoreType.DMA((8,)),
        ],
        compiler_params=pltpu.CompilerParams(
            collective_id=0, has_side_effects=True, vmem_limit_bytes=60 * 1024 * 1024),
        name="attention_backward",
    )(seen, source, rows, queries, output_cotangent, keys, values)
    return tuple(outs)


def solution(mesh):
    rows = P(("rail", "node"), None)
    return jax.shard_map(
        per_device, mesh=mesh, in_specs=(rows, rows, rows, rows, P(), P()),
        out_specs=(rows, rows, rows), check_vma=False,
    )
```

```python
import math

import jax
import jax.numpy as jnp
from jax import lax
from jax.experimental import pallas as pl
from jax.experimental.pallas import tpu as pltpu
from jax.sharding import PartitionSpec as P

HEAD = 128
SPAN = 128
NX, NZ, NY, NC = 4, 8, 4, 2
ROWS = 64
BLOCK = NX * ROWS
SLOTS = 4
NSLOT = NZ * NY * SLOTS
QHEADS = 4
LANES = QHEADS * SPAN
WIDE = QHEADS * HEAD
STEP = 256
STEPS = 9
WIN = STEP * STEPS
WT = WIN // SPAN
HALF = SPAN // 2
FAR = NZ // 2
SCALE = 1.0 / math.sqrt(HEAD)
C2 = SCALE * 1.4426950408889634
NEG = -1e30
MESH = pl.DeviceIdType.MESH
F32 = jnp.float32
BF16 = jnp.bfloat16
N_RECV = 208
N_SEND = 5
RULER = 126
COLUMNS = [0, 1, -1, 2, -2, 3, -3, 4]


class Place:
    def __init__(self):
        self.x = lax.axis_index("node")
        rail = lax.axis_index("rail")
        self.c = rail % NC
        self.y = (rail // NC) % NY
        self.z = rail // (NC * NY)

    def at(self, x=None, z=None, y=None, c=None):
        x = self.x if x is None else x
        z = self.z if z is None else z
        y = self.y if y is None else y
        c = self.c if c is None else c
        return (x, (z * NY + y) * NC + c)

    def zz(self, d):
        return (self.z + d + NZ) % NZ

    def yy(self, d):
        return (self.y + d + NY) % NY

    def ring(self, axis, step):
        return self.at(z=self.zz(step)) if axis == "z" else self.at(y=self.yy(step))

    def sibling(self):
        return self.at(c=1 - self.c)

    def team(self):
        out = []
        for step in range(1, NX * NC):
            j = (self.x * NC + self.c + step) % (NX * NC)
            out.append((j, self.at(x=j // NC, c=j % NC)))
        return out


def greet(place):
    barrier = pltpu.get_barrier_semaphore()
    peers = [dev for _, dev in place.team()]
    peers += [place.ring("z", 1), place.ring("z", -1)]
    peers += [place.ring("y", k) for k in range(1, NY)]
    for dev in peers:
        pl.semaphore_signal(barrier, inc=1, device_id=dev, device_id_type=MESH)
    pl.semaphore_wait(barrier, len(peers))


class Copies:
    def __init__(self, send, recv, ruler):
        self.send, self.recv, self.ruler, self.count = send, recv, ruler, 0

    def slot(self):
        self.count += 1
        return self.count - 1

    def make(self, src, dst, dev, group, slot=None):
        slot = self.slot() if slot is None else slot
        return pltpu.make_async_remote_copy(
            src_ref=src, dst_ref=dst, send_sem=self.send.at[group], recv_sem=self.recv.at[slot],
            device_id=dev, device_id_type=MESH,
        )

    def size(self, spans, rows=SPAN):
        return self.ruler.at[pl.ds(0, spans), pl.ds(0, rows), :]

    def arrived(self, slot, spans, rows=SPAN):
        ref = self.size(spans, rows)
        pltpu.make_async_copy(ref, ref, self.recv.at[slot]).wait()

    def sent(self, group, spans):
        ref = self.size(spans)
        pltpu.make_async_copy(ref, ref, self.send.at[group]).wait()


def line(z, c, b):
    return ((z * NC + c) * 2 + b) * NY


class Gather:
    def __init__(self, me, cp, ref, group):
        self.cp, self.ref, self.group = cp, ref, group
        c, y = me.c, me.y

        def blk(zi, yi, b, lo=0, n=SPAN):
            return ref.at[line(zi, c, b) + yi, pl.ds(lo, n), :]

        def make(src, dev, slot=None):
            return cp.make(src, src, dev, group, slot)

        self.z = [{}, {}]
        self.z2 = [[{} for _ in range(NY)] for _ in range(2)]
        for d in range(1, FAR + 1):
            for i, sign in enumerate((1, -1)):
                lo, n = (i * HALF, HALF) if d == FAR else (0, SPAN)
                zi = me.zz(-sign * (d - 1))
                to = me.ring("z", sign)
                self.z[i][d] = make(blk(zi, y, 0, lo, n), to)
                for k in range(NY):
                    self.z2[i][k][d] = make(blk(zi, me.yy(k), 1, lo, n), to)
        self.y, self.y_slot = {}, {}
        for d in COLUMNS:
            self.y_slot[d] = cp.slot()
            src = blk(me.zz(d), y, 0)
            self.y[d] = [make(src, me.ring("y", k), self.y_slot[d]) for k in range(1, NY)]
        src = blk(me.z, y, 1)
        self.y2 = [make(src, me.ring("y", k)) for k in range(1, NY)]
        self.sib = [{}, {}]
        self.sib_slot = cp.slot()
        for d in COLUMNS:
            for b in range(2):
                src = ref.at[pl.ds(line(me.zz(d), c, b), NY)]
                self.sib[b][d] = make(src, me.sibling(), self.sib_slot)

    def begin(self):
        for i in range(2):
            self.z[i][1].start()
        for copy in self.y2:
            copy.start()
        for i in range(2):
            self.z2[i][0][1].start()
        for copy in self.y[0]:
            copy.start()

    def second(self):
        for k in range(1, NY):
            self.y2[k - 1].wait_recv()
            for i in range(2):
                self.z2[i][NY - k][1].start()
        self.sib[1][0].start()

    def near(self, d):
        for i, sign in enumerate((1, -1)):
            self.z[i][d].wait_recv()
            if d < FAR:
                self.z[i][d + 1].start()
                for copy in self.y[-sign * d]:
                    copy.start()
        if d == FAR:
            for copy in self.y[FAR]:
                copy.start()

    def wide(self, d):
        for k in (0, 3, 2, 1):
            for i in range(2):
                self.z2[i][k][d].wait_recv()
                if d < FAR:
                    self.z2[i][k][d + 1].start()
        self.sib[1][d].start()
        if d < FAR:
            self.sib[1][-d].start()

    def finish(self, *cols):
        for d in cols:
            self.cp.arrived(self.y_slot[d], NY - 1)
            self.sib[0][d].start()

    def done(self):
        self.cp.arrived(self.sib_slot, NSLOT // 2)

    def drain(self):
        self.cp.sent(self.group, RULER)


def add(dst, *srcs):
    total = dst[...].astype(F32)
    for src in srcs:
        total = total + src[...].astype(F32)
    dst[...] = total.astype(BF16)


class Scatter:
    def __init__(self, me, cp, window, source, bufs, group):
        self.me, self.cp, self.window, self.source, self.group = me, cp, window, source, group
        (self.acc, self.snd, self.sibr, self.yr, self.yr1,
         self.zr0h, self.zr0f, self.zr1h, self.zr1f) = bufs
        acc, y = self.acc, me.y
        self.sib, self.y0, self.y0_slot = {}, {}, {}

        def make(src, dst, dev, slot=None):
            return cp.make(src, dst, dev, group, slot)

        for i, d in enumerate(COLUMNS):
            self.sib[d] = make(self.snd.at[me.zz(d)], self.sibr.at[me.zz(d)], me.sibling())
            self.y0_slot[d] = cp.slot()
            self.y0[d] = [
                make(acc.at[me.zz(d), me.yy(k), 0], self.yr.at[i, k - 1], me.ring("y", k),
                     self.y0_slot[d])
                for k in range(1, NY)
            ]
        self.y1_slot = cp.slot()
        self.y1 = [
            make(acc.at[me.z, me.yy(k), 1], self.yr1.at[k - 1], me.ring("y", k), self.y1_slot)
            for k in range(1, NY)
        ]
        self.z0 = [{}, {}]
        self.z1 = [[{}, {}], [{}, {}]]
        for d in range(FAR, 0, -1):
            for i, sign in enumerate((1, -1)):
                to = me.ring("z", sign)
                zi = me.zz(sign * d)
                rows = pl.ds(i * HALF, HALF) if d == FAR else pl.ds(0, SPAN)
                dst = self.zr0h.at[i] if d == FAR else self.zr0f.at[d - 1, i]
                self.z0[i][d] = make(acc.at[zi, y, 0, rows, :], dst, to)
                for h in range(2):
                    ys = pl.ds(2 * h, 2)
                    dst = self.zr1h.at[i, ys] if d == FAR else self.zr1f.at[d - 1, i, ys]
                    self.z1[i][h][d] = make(acc.at[zi, ys, 1, rows, :], dst, to)

    def drain(self):
        self.cp.sent(self.group, RULER)

    def collect(self, d):
        me = self.me
        zi = me.zz(d)

        def tiles(core, dst):
            def body(i, _):
                yi, b = i // 2, i % 2
                j = line(zi, core, b) + yi
                total = None
                for s in range(SLOTS):
                    w = self.source[s * NSLOT + j]
                    tile = self.window[w]
                    total = tile if total is None else total + tile
                dst[zi, yi, b] = total
                return 0
            lax.fori_loop(0, NY * 2, body, 0, unroll=8)

        tiles(1 - me.c, self.snd)
        self.sib[d].start()
        tiles(me.c, self.acc)

    def pair(self, *cols):
        me = self.me
        for d in cols:
            zi = me.zz(d)
            self.sib[d].wait_recv()

            def body(yi, _):
                add(self.acc.at[zi, yi], self.sibr.at[zi, yi])
                return 0

            lax.fori_loop(0, NY, body, 0)
            for copy in self.y0[d]:
                copy.start()
            if d == FAR:
                for h in range(2):
                    for i in range(2):
                        self.z1[i][h][d].start()

    def yadd(self, *cols):
        me = self.me
        for d in cols:
            j = COLUMNS.index(d)
            self.cp.arrived(self.y0_slot[d], NY - 1)
            add(self.acc.at[me.zz(d), me.y, 0], *[self.yr.at[j, k] for k in range(NY - 1)])
            if d == FAR:
                for i in range(2):
                    self.z0[i][d].start()

    def z0step(self, d):
        me = self.me
        for i, sign in enumerate((1, -1)):
            self.z0[i][d + 1].wait_recv()
            zi = me.zz(sign * d)
            if d == FAR - 1:
                add(self.acc.at[zi, me.y, 0, pl.ds(i * HALF, HALF), :], self.zr0h.at[i])
            else:
                add(self.acc.at[zi, me.y, 0], self.zr0f.at[d, i])
            self.z0[i][d].start()

    def z1step(self, d):
        me = self.me
        for h in range(2):
            for i, sign in enumerate((1, -1)):
                self.z1[i][h][d + 1].wait_recv()
                zi = me.zz(sign * d)
                for yi in range(2 * h, 2 * h + 2):
                    if d == FAR - 1:
                        add(self.acc.at[zi, yi, 1, pl.ds(i * HALF, HALF), :], self.zr1h.at[i, yi])
                    else:
                        add(self.acc.at[zi, yi, 1], self.zr1f.at[d, i, yi])
                self.z1[i][h][d].start()

    def z1last(self):
        me = self.me
        for h in range(2):
            for i in range(2):
                self.z1[i][h][1].wait_recv()
            for yi in range(2 * h, 2 * h + 2):
                add(self.acc.at[me.z, yi, 1], self.zr1f.at[0, 0, yi], self.zr1f.at[0, 1, yi])
        for copy in self.y1:
            copy.start()

    def z0last(self):
        me = self.me
        for i in range(2):
            self.z0[i][1].wait_recv()
        add(self.acc.at[me.z, me.y, 0], self.zr0f.at[0, 0], self.zr0f.at[0, 1])

    def y1last(self):
        me = self.me
        self.cp.arrived(self.y1_slot, NY - 1)
        add(self.acc.at[me.z, me.y, 1], *[self.yr1.at[k] for k in range(NY - 1)])


def fold(x, op):
    return op(x.reshape(x.shape[0] // 8, 8, x.shape[1]), axis=0)


def at_step(t):
    return pl.ds(t * STEP, STEP)


def span_rows(i):
    return pl.ds(pl.multiple_of(i * SPAN, SPAN), SPAN)


def load_window(s, seen, src, put):
    def body(w, _):
        j = seen[s * WT + w]
        put(w, src[j])
        return 0

    lax.fori_loop(0, WT, body, 0, unroll=2)


def tables_kernel(slot_ref, len_ref, seen, source, rows_ref, span_of):
    chip = lax.axis_index("rail") // NC

    def invert(i, _):
        span_of[slot_ref[i]] = i
        return 0

    lax.fori_loop(0, NSLOT, invert, 0, unroll=16)
    for s in range(SLOTS):
        def clear(i, _):
            source[s * NSLOT + i] = s * WT
            return 0

        lax.fori_loop(0, NSLOT, clear, 0, unroll=32)

    row = lax.broadcasted_iota(jnp.int32, (8, LANES), 0)
    span_rows_ = jnp.zeros((8, LANES), jnp.int32)
    for s in range(SLOTS):
        span = span_of[chip * SLOTS + s]
        span_rows_ = jnp.where(row == s, span, span_rows_)
        seen[s * WT] = 0
        for w in range(1, WT):
            n = span - (WT - 1) + w
            j = slot_ref[jnp.maximum(n, 0)]
            j = (j & ~15) | ((j & 3) << 2) | ((j >> 2) & 3)
            seen[s * WT + w] = j
            source[jnp.where(n >= 0, s * NSLOT + j, SLOTS * NSLOT)] = s * WT + w
    lane = lax.broadcasted_iota(jnp.int32, (8, LANES), 1) % SPAN
    qpos = span_rows_ * SPAN + lane
    qstart = jnp.zeros((8, LANES), jnp.int32)
    end = 0
    for i in range(len_ref.shape[0]):
        end = end + len_ref[i]
        qstart = jnp.where(qpos >= end, end, qstart)
    rows_ref[0] = qstart - (span_rows_ - (WT - 1)) * SPAN
    rows_ref[1] = qpos - qstart


def kernel(seen, source, rows_ref, q_ref, o_ref, k_ref, v_ref, dq_ref, dk_ref, dv_ref,
           k_all, v_all, qm, om, kw, vw, qs, os_, tq, s_scr, p_scr, wk, wv, inv_scr, dqm,
           *rest):
    bufs_v, bufs_k = rest[:9], rest[9:18]
    send, recv, local = rest[18:]
    me = Place()
    cp = Copies(send, recv, k_all)
    x, z, y, c = me.x, me.z, me.y, me.c
    j_me = x * NC + c

    def cols(j, n):
        return pl.ds(pl.multiple_of(j * n, n), n)

    kvx = [[], []]
    own = []
    mine = pl.ds(pl.multiple_of((x % 2) * ROWS, ROWS), ROWS)
    kvx_slot = [cp.slot(), cp.slot()]
    for i, (src, dst) in enumerate(((k_ref, k_all), (v_ref, v_all))):
        for step in range(1, NX):
            to = (x + step) % NX
            kvx[i].append(cp.make(
                src.at[:, cols(to, HEAD)], dst.at[line(z, c, x // 2) + y, mine, :], me.at(x=to),
                0, kvx_slot[i]))
        own.append(pltpu.make_async_copy(
            src.at[:, cols(x, HEAD)], dst.at[line(z, c, x // 2) + y, mine, :], local.at[i]))
    rows = pl.ds(pl.multiple_of(c * BLOCK + x * ROWS, ROWS), ROWS)
    qo = [[], []]
    qo_slot = [cp.slot(), cp.slot()]
    for i, (src, dst) in enumerate(((q_ref, qm), (o_ref, om))):
        for j, dev in me.team():
            qo[i].append(cp.make(
                src.at[:, cols(j, WIDE)], dst.at[rows, :], dev, 0, qo_slot[i]))
        own.append(pltpu.make_async_copy(
            src.at[:, cols(j_me, WIDE)], dst.at[rows, :], local.at[2 + i]))
    gk, gv = Gather(me, cp, k_all, 1), Gather(me, cp, v_all, 2)
    sv = Scatter(me, cp, wv, source, bufs_v, 3)
    sk = Scatter(me, cp, wk, source, bufs_k, 4)
    dqs = []
    dqs_slot = cp.slot()
    for j, dev in me.team():
        there = pl.ds(pl.multiple_of((j % NC) * BLOCK + (j // NC) * ROWS, ROWS), ROWS)
        dqs.append(cp.make(
            dqm.at[there, :], dq_ref.at[:, cols(j_me, WIDE)], dev, 0, dqs_slot))
    own.append(pltpu.make_async_copy(dqm.at[rows, :], dq_ref.at[:, cols(j_me, WIDE)], local.at[4]))
    back = [[], []]
    back_slot = [cp.slot(), cp.slot()]
    for i, (acc, dst) in enumerate(((bufs_k[0], dk_ref), (bufs_v[0], dv_ref))):
        for step in range(1, NX):
            to = (x + step) % NX
            part = pl.ds(pl.multiple_of((to % 2) * ROWS, ROWS), ROWS)
            back[i].append(cp.make(
                acc.at[z, y, to // 2, part, :], dst.at[:, cols(x, HEAD)], me.at(x=to),
                0, back_slot[i]))
        own.append(pltpu.make_async_copy(
            acc.at[z, y, x // 2, mine, :], dst.at[:, cols(x, HEAD)], local.at[5 + i]))
    assert cp.count <= N_RECV

    greet(me)
    for i in range(2):
        for copy in kvx[i]:
            copy.start()
        own[i].start()
    cp.arrived(kvx_slot[0], NX - 1, ROWS)
    own[0].wait()
    gk.begin()
    for i in range(2):
        for copy in qo[i]:
            copy.start()
        own[2 + i].start()
    gk.near(1)
    gk.second()
    gk.finish(0)
    gk.near(2)
    gk.wide(1)
    gk.finish(1, -1)
    cp.arrived(kvx_slot[1], NX - 1, ROWS)
    own[1].wait()
    gv.begin()
    gk.near(3)
    gk.wide(2)
    gk.finish(2, -2)
    gv.near(1)
    gv.second()
    gk.near(4)
    gk.wide(3)
    gv.near(2)
    gv.finish(0)
    gk.finish(3, -3)
    gk.finish(4)
    gv.wide(1)
    gv.finish(1, -1)
    gk.wide(4)
    gk.done()
    for i in range(2):
        cp.arrived(qo_slot[i], 14)
        own[2 + i].wait()

    sub = lax.broadcasted_iota(jnp.int32, (STEP, 1), 0)

    def during(s, table):
        for i, events in enumerate(table):
            if events:
                @pl.when(s == i)
                def _():
                    for event in events:
                        event()

    def first_part(s, _):
        low, extra = rows_ref[0, pl.ds(s, 1), :], rows_ref[1, pl.ds(s, 1), :]

        def put(w, tile):
            kw[s, span_rows(w), :] = tile

        load_window(s, seen, k_all, put)
        for h in range(QHEADS):
            qh = qm[span_rows(s), h * HEAD:(h + 1) * HEAD]
            qs[s, h * SPAN:(h + 1) * SPAN, :] = qh
            tq[:, h * SPAN:(h + 1) * SPAN] = qh.T
        top = jnp.full((8, LANES), NEG, F32)
        for t in range(STEPS):
            st = jnp.dot(kw[s, at_step(t), :], tq[...], preferred_element_type=F32)
            rel = (sub + t * STEP) - low
            st = jnp.where((rel >= 0) & (rel <= extra), st, NEG)
            s_scr[t] = st
            top = jnp.maximum(top, fold(st, jnp.max))
        during(s, v_events[0])
        mc = jnp.max(top, axis=0, keepdims=True) * C2
        total = jnp.zeros((8, LANES), F32)
        for t in range(STEPS):
            p = jnp.exp2(s_scr[t] * C2 - mc)
            p_scr[s, t] = p.astype(BF16)
            total = total + fold(p, jnp.sum)
        inv = 1.0 / jnp.sum(total, axis=0, keepdims=True)
        inv8 = jnp.broadcast_to(inv, (8, LANES))
        inv_scr[s] = inv8
        for h in range(QHEADS):
            col = inv8[:, h * SPAN:(h + 1) * SPAN].T[:, :1]
            oh = om[span_rows(s), h * HEAD:(h + 1) * HEAD].astype(F32)
            os_[s, h * SPAN:(h + 1) * SPAN, :] = (oh * col).astype(BF16)
        during(s, v_events[1])
        for t in range(STEPS):
            dv = jnp.dot(p_scr[s, t], os_[s], preferred_element_type=F32)
            wv[pl.ds(s * WT + 2 * t, 2)] = dv.astype(BF16).reshape(2, SPAN, HEAD)
        during(s, v_events[2])
        return 0

    v_events = [
        [[lambda: gv.near(3)], [lambda: gv.near(4)], [lambda: gv.finish(4)], None],
        [[lambda: gv.wide(2)], [lambda: gv.wide(3)], [lambda: gv.wide(4)], None],
        [[lambda: gv.finish(2, -2)], [lambda: gv.finish(3, -3)], None, None],
    ]
    lax.fori_loop(0, SLOTS, first_part, 0)
    gv.done()

    sv.collect(4)
    sv.collect(3)
    sv.pair(4)
    sv.collect(-3)
    sv.pair(3)

    def second_part(s, _):

        def put(w, tile):
            vw[span_rows(w), :] = tile

        load_window(s, seen, v_all, put)
        for h in range(QHEADS):
            tq[:, h * SPAN:(h + 1) * SPAN] = os_[s, h * SPAN:(h + 1) * SPAN, :].T
        total = jnp.zeros((8, LANES), F32)
        for t in range(STEPS):
            dp = jnp.dot(vw[at_step(t), :], tq[...], preferred_element_type=F32)
            s_scr[t] = dp
            total = total + fold(p_scr[s, t].astype(F32) * dp, jnp.sum)
        during(s, k_events[0])
        dots = jnp.sum(total, axis=0, keepdims=True) * inv_scr[s, :1, :]
        for t in range(STEPS):
            ds = (p_scr[s, t].astype(F32) * (s_scr[t] - dots)).astype(BF16)
            p_scr[s, t] = ds
            dk = jnp.dot(ds, qs[s], preferred_element_type=F32) * SCALE
            wk[pl.ds(s * WT + 2 * t, 2)] = dk.astype(BF16).reshape(2, SPAN, HEAD)
        during(s, k_events[1])
        return 0

    def third_part(s, _):
        total = jnp.zeros((HEAD, LANES), F32)
        for t in range(STEPS):
            total = total + lax.dot_general(kw[s, at_step(t), :], p_scr[s, t],
                                            (((0,), (0,)), ((), ())), preferred_element_type=F32)
        for h in range(QHEADS):
            dqm[span_rows(s), h * HEAD:(h + 1) * HEAD] = (
                (total[:, h * SPAN:(h + 1) * SPAN] * SCALE).T.astype(BF16))
        during(s, q_events)
        return 0

    k_events = [
        [
            [lambda: sv.collect(2), lambda: sv.pair(-3), lambda: sv.collect(-2)],
            [lambda: sv.yadd(4), lambda: sv.collect(1), lambda: sv.collect(-1)],
            [lambda: sv.z1step(2), lambda: sv.pair(1, -1)],
            [lambda: sv.z0step(2), lambda: sv.z1step(1)],
        ],
        [
            [lambda: sv.z1step(3), lambda: sv.pair(2, -2)],
            [lambda: sv.yadd(3, -3), lambda: sv.z0step(3), lambda: sv.collect(0)],
            [lambda: sv.yadd(2, -2), lambda: sv.pair(0)],
            [lambda: sv.yadd(1, -1)],
        ],
    ]
    lax.fori_loop(0, SLOTS, second_part, 0)

    sk.collect(4)
    sk.collect(3)
    sv.z0step(1)
    sk.pair(4)
    sk.collect(-3)
    sv.z1last()
    sk.pair(3)
    sk.collect(2)
    sk.pair(-3)
    sk.collect(-2)
    sk.z1step(3)
    sk.pair(2, -2)
    sv.yadd(0)
    sv.z0last()
    sk.yadd(4)
    sk.collect(1)
    sk.collect(-1)
    sv.y1last()
    for copy in back[1]:
        copy.start()
    own[6].start()
    sk.yadd(3, -3)
    q_events = [
        [lambda: sk.z0step(3), lambda: sk.z1step(2), lambda: sk.pair(1, -1)],
        [lambda: sk.collect(0), lambda: sk.yadd(2, -2)],
        [lambda: sk.z0step(2), lambda: sk.pair(0)],
        [lambda: sk.z1step(1), lambda: sk.yadd(1, -1)],
    ]
    lax.fori_loop(0, SLOTS, third_part, 0)
    for copy in dqs:
        copy.start()
    own[4].start()
    sk.z0step(1)
    sk.yadd(0)
    sk.z1last()
    gk.drain()
    gv.drain()
    sv.drain()
    sk.z0last()
    sk.y1last()
    for copy in back[0]:
        copy.start()
    own[5].start()
    sk.drain()
    cp.arrived(dqs_slot, 14)
    for i in range(2):
        cp.arrived(back_slot[i], NX - 1, ROWS)
    cp.sent(0, 48)
    for i in (4, 5, 6):
        own[i].wait()


def settle_kernel(dq_in, dk_in, dv_in, dq_out, dk_out, dv_out):
    dq_out[...] = dq_in[...]
    dk_out[...] = dk_in[...]
    dv_out[...] = dv_in[...]


def per_device(queries, keys, values, output_cotangent, doc_lengths, span_slot):
    smem = pl.BlockSpec(memory_space=pltpu.SMEM)
    any_spec = pl.BlockSpec(memory_space=pl.ANY)

    def vmem(*shape, dtype=BF16):
        return pltpu.VMEM(shape, dtype)

    scatter_bufs = [
        vmem(NZ, NY, 2, SPAN, HEAD),
        vmem(NZ, NY, 2, SPAN, HEAD),
        vmem(NZ, NY, 2, SPAN, HEAD),
        vmem(NZ, NY - 1, SPAN, HEAD),
        vmem(NY - 1, SPAN, HEAD),
        vmem(2, HALF, HEAD),
        vmem(FAR - 1, 2, SPAN, HEAD),
        vmem(2, NY, HALF, HEAD),
        vmem(FAR - 1, 2, NY, SPAN, HEAD),
    ]
    seen, source, rows = pl.pallas_call(
        tables_kernel,
        out_shape=[
            jax.ShapeDtypeStruct((SLOTS * WT,), jnp.int32),
            jax.ShapeDtypeStruct((SLOTS * NSLOT + 8,), jnp.int32),
            jax.ShapeDtypeStruct((2, 8, LANES), jnp.int32),
        ],
        in_specs=[smem] * 2,
        out_specs=[smem, smem, pl.BlockSpec(memory_space=pltpu.VMEM)],
        scratch_shapes=[pltpu.SMEM((NSLOT,), jnp.int32)],
        name="tables",
    )(span_slot, doc_lengths)
    outs = pl.pallas_call(
        kernel,
        out_shape=[
            jax.ShapeDtypeStruct(queries.shape, BF16),
            jax.ShapeDtypeStruct(keys.shape, BF16),
            jax.ShapeDtypeStruct(values.shape, BF16),
        ],
        in_specs=[smem] * 2 + [pl.BlockSpec(memory_space=pltpu.VMEM)] + [any_spec] * 4,
        out_specs=[any_spec] * 3,
        scratch_shapes=[
            vmem(NSLOT, SPAN, HEAD),
            vmem(NSLOT, SPAN, HEAD),
            vmem(SLOTS * SPAN, WIDE),
            vmem(SLOTS * SPAN, WIDE),
            vmem(SLOTS, WIN, HEAD),
            vmem(WIN, HEAD),
            vmem(SLOTS, LANES, HEAD),
            vmem(SLOTS, LANES, HEAD),
            vmem(HEAD, LANES),
            vmem(STEPS, STEP, LANES, dtype=F32),
            vmem(SLOTS, STEPS, STEP, LANES),
            vmem(SLOTS * WT, SPAN, HEAD),
            vmem(SLOTS * WT, SPAN, HEAD),
            vmem(SLOTS, 8, LANES, dtype=F32),
            vmem(SLOTS * SPAN, WIDE),
        ] + scatter_bufs * 2 + [
            pltpu.SemaphoreType.DMA((N_SEND,)),
            pltpu.SemaphoreType.DMA((N_RECV,)),
            pltpu.SemaphoreType.DMA((8,)),
        ],
        compiler_params=pltpu.CompilerParams(
            collective_id=0, has_side_effects=True, vmem_limit_bytes=60 * 1024 * 1024),
        name="attention_backward",
    )(seen, source, rows, queries, output_cotangent, keys, values)
    outs = pl.pallas_call(
        settle_kernel,
        out_shape=[jax.ShapeDtypeStruct(out.shape, out.dtype) for out in outs],
        in_specs=[pl.BlockSpec(memory_space=pltpu.VMEM)] * 3,
        out_specs=[pl.BlockSpec(memory_space=pltpu.VMEM)] * 3,
        name="settle",
    )(*outs)
    return tuple(outs)


def solution(mesh):
    rows = P(("rail", "node"), None)
    return jax.shard_map(
        per_device, mesh=mesh, in_specs=(rows, rows, rows, rows, P(), P()),
        out_specs=(rows, rows, rows), check_vma=False,
    )
```

```python
import math

import jax
import jax.numpy as jnp
from jax import lax
from jax.experimental import pallas as pl
from jax.experimental.pallas import tpu as pltpu
from jax.sharding import PartitionSpec as P

HEAD = 128
SPAN = 128
NX, NZ, NY, NC = 4, 8, 4, 2
ROWS = 64
BLOCK = NX * ROWS
SLOTS = 4
NSLOT = NZ * NY * SLOTS
QHEADS = 4
LANES = QHEADS * SPAN
WIDE = QHEADS * HEAD
WT = 17
HALF = SPAN // 2
FAR = NZ // 2
SCALE = 1.0 / math.sqrt(HEAD)
C2 = SCALE * 1.4426950408889634
NEG = -1e30
MESH = pl.DeviceIdType.MESH
F32 = jnp.float32
BF16 = jnp.bfloat16
N_RECV = 208
N_SEND = 5
RULER = 126
COLUMNS = [0, 1, -1, 2, -2, 3, -3, 4]


class Place:
    def __init__(self):
        self.x = lax.axis_index("node")
        rail = lax.axis_index("rail")
        self.c = rail % NC
        self.y = (rail // NC) % NY
        self.z = rail // (NC * NY)

    def at(self, x=None, z=None, y=None, c=None):
        x = self.x if x is None else x
        z = self.z if z is None else z
        y = self.y if y is None else y
        c = self.c if c is None else c
        return (x, (z * NY + y) * NC + c)

    def zz(self, d):
        return (self.z + d + NZ) % NZ

    def yy(self, d):
        return (self.y + d + NY) % NY

    def ring(self, axis, step):
        return self.at(z=self.zz(step)) if axis == "z" else self.at(y=self.yy(step))

    def sibling(self):
        return self.at(c=1 - self.c)

    def team(self):
        out = []
        for step in range(1, NX * NC):
            j = (self.x * NC + self.c + step) % (NX * NC)
            out.append((j, self.at(x=j // NC, c=j % NC)))
        return out


def greet(place):
    barrier = pltpu.get_barrier_semaphore()
    peers = [dev for _, dev in place.team()]
    peers += [place.ring("z", 1), place.ring("z", -1)]
    peers += [place.ring("y", k) for k in range(1, NY)]
    for dev in peers:
        pl.semaphore_signal(barrier, inc=1, device_id=dev, device_id_type=MESH)
    pl.semaphore_wait(barrier, len(peers))


class Copies:
    def __init__(self, send, recv, ruler):
        self.send, self.recv, self.ruler, self.count = send, recv, ruler, 0

    def slot(self):
        self.count += 1
        return self.count - 1

    def make(self, src, dst, dev, group, slot=None):
        slot = self.slot() if slot is None else slot
        return pltpu.make_async_remote_copy(
            src_ref=src, dst_ref=dst, send_sem=self.send.at[group], recv_sem=self.recv.at[slot],
            device_id=dev, device_id_type=MESH,
        )

    def size(self, spans, rows=SPAN):
        return self.ruler.at[pl.ds(0, spans), pl.ds(0, rows), :]

    def arrived(self, slot, spans, rows=SPAN):
        ref = self.size(spans, rows)
        pltpu.make_async_copy(ref, ref, self.recv.at[slot]).wait()

    def sent(self, group, spans):
        ref = self.size(spans)
        pltpu.make_async_copy(ref, ref, self.send.at[group]).wait()


def line(z, c, b):
    return ((z * NC + c) * 2 + b) * NY


class Gather:
    def __init__(self, me, cp, ref, group):
        self.cp, self.ref, self.group = cp, ref, group
        c, y = me.c, me.y

        def blk(zi, yi, b, lo=0, n=SPAN):
            return ref.at[line(zi, c, b) + yi, pl.ds(lo, n), :]

        def make(src, dev, slot=None):
            return cp.make(src, src, dev, group, slot)

        self.z = [{}, {}]
        self.z2 = [[{} for _ in range(NY)] for _ in range(2)]
        for d in range(1, FAR + 1):
            for i, sign in enumerate((1, -1)):
                lo, n = (i * HALF, HALF) if d == FAR else (0, SPAN)
                zi = me.zz(-sign * (d - 1))
                to = me.ring("z", sign)
                self.z[i][d] = make(blk(zi, y, 0, lo, n), to)
                for k in range(NY):
                    self.z2[i][k][d] = make(blk(zi, me.yy(k), 1, lo, n), to)
        self.y, self.y_slot = {}, {}
        for d in COLUMNS:
            self.y_slot[d] = cp.slot()
            src = blk(me.zz(d), y, 0)
            self.y[d] = [make(src, me.ring("y", k), self.y_slot[d]) for k in range(1, NY)]
        src = blk(me.z, y, 1)
        self.y2 = [make(src, me.ring("y", k)) for k in range(1, NY)]
        self.sib = [{}, {}]
        self.sib_slot = cp.slot()
        for d in COLUMNS:
            for b in range(2):
                src = ref.at[pl.ds(line(me.zz(d), c, b), NY)]
                self.sib[b][d] = make(src, me.sibling(), self.sib_slot)

    def begin(self):
        for i in range(2):
            self.z[i][1].start()
        for copy in self.y2:
            copy.start()
        for i in range(2):
            self.z2[i][0][1].start()
        for copy in self.y[0]:
            copy.start()

    def second(self):
        for k in range(1, NY):
            self.y2[k - 1].wait_recv()
            for i in range(2):
                self.z2[i][NY - k][1].start()
        self.sib[1][0].start()

    def near(self, d):
        for i, sign in enumerate((1, -1)):
            self.z[i][d].wait_recv()
            if d < FAR:
                self.z[i][d + 1].start()
                for copy in self.y[-sign * d]:
                    copy.start()
        if d == FAR:
            for copy in self.y[FAR]:
                copy.start()

    def wide(self, d, half):
        for k in ((0, 3), (2, 1))[half]:
            for i in range(2):
                self.z2[i][k][d].wait_recv()
                if d < FAR:
                    self.z2[i][k][d + 1].start()
        if half:
            self.sib[1][d].start()
            if d < FAR:
                self.sib[1][-d].start()

    def finish(self, *cols):
        for d in cols:
            self.cp.arrived(self.y_slot[d], NY - 1)
            self.sib[0][d].start()

    def done(self):
        self.cp.arrived(self.sib_slot, NSLOT // 2)

    def drain(self):
        self.cp.sent(self.group, RULER)


def add(dst, *srcs):
    if len(srcs) == 1:
        dst[...] += srcs[0][...]
        return
    total = dst[...].astype(F32)
    for src in srcs:
        total = total + src[...].astype(F32)
    dst[...] = total.astype(BF16)


class Scatter:
    def __init__(self, me, cp, window, source, bufs, group):
        self.me, self.cp, self.window, self.source, self.group = me, cp, window, source, group
        (self.acc, self.snd, self.sibr, self.yr, self.yr1,
         self.zr0h, self.zr0f, self.zr1h, self.zr1f) = bufs
        acc, y = self.acc, me.y
        self.sib, self.y0, self.y0_slot = {}, {}, {}

        def make(src, dst, dev, slot=None):
            return cp.make(src, dst, dev, group, slot)

        for i, d in enumerate(COLUMNS):
            self.sib[d] = make(self.snd.at[me.zz(d)], self.sibr.at[me.zz(d)], me.sibling())
            self.y0_slot[d] = cp.slot()
            self.y0[d] = [
                make(acc.at[me.zz(d), me.yy(k), 0], self.yr.at[i, k - 1], me.ring("y", k),
                     self.y0_slot[d])
                for k in range(1, NY)
            ]
        self.y1_slot = cp.slot()
        self.y1 = [
            make(acc.at[me.z, me.yy(k), 1], self.yr1.at[k - 1], me.ring("y", k), self.y1_slot)
            for k in range(1, NY)
        ]
        self.z0 = [{}, {}]
        self.z1 = [[{}, {}], [{}, {}]]
        for d in range(FAR, 0, -1):
            for i, sign in enumerate((1, -1)):
                to = me.ring("z", sign)
                zi = me.zz(sign * d)
                rows = pl.ds(i * HALF, HALF) if d == FAR else pl.ds(0, SPAN)
                dst = self.zr0h.at[i] if d == FAR else self.zr0f.at[d - 1, i]
                self.z0[i][d] = make(acc.at[zi, y, 0, rows, :], dst, to)
                for h in range(2):
                    ys = pl.ds(2 * h, 2)
                    dst = self.zr1h.at[i, ys] if d == FAR else self.zr1f.at[d - 1, i, ys]
                    self.z1[i][h][d] = make(acc.at[zi, ys, 1, rows, :], dst, to)

    def drain(self):
        self.cp.sent(self.group, RULER)

    def collect(self, d):
        me = self.me
        zi = me.zz(d)

        def tiles(core, dst):
            def body(i, _):
                yi, b = i // 2, i % 2
                j = line(zi, core, b) + yi
                total = None
                for s in range(SLOTS):
                    w = self.source[s * NSLOT + j]
                    tile = self.window[w]
                    total = tile if total is None else total + tile
                dst[zi, yi, b] = total
                return 0
            lax.fori_loop(0, NY * 2, body, 0, unroll=8)

        tiles(1 - me.c, self.snd)
        self.sib[d].start()
        tiles(me.c, self.acc)

    def pair(self, *cols):
        me = self.me
        for d in cols:
            zi = me.zz(d)
            self.sib[d].wait_recv()

            add(self.acc.at[zi], self.sibr.at[zi])
            for copy in self.y0[d]:
                copy.start()
            if d == FAR:
                for h in range(2):
                    for i in range(2):
                        self.z1[i][h][d].start()

    def yadd(self, *cols):
        me = self.me
        for d in cols:
            j = COLUMNS.index(d)
            self.cp.arrived(self.y0_slot[d], NY - 1)
            add(self.acc.at[me.zz(d), me.y, 0], *[self.yr.at[j, k] for k in range(NY - 1)])
            if d == FAR:
                for i in range(2):
                    self.z0[i][d].start()

    def z0step(self, d):
        me = self.me
        for i, sign in enumerate((1, -1)):
            self.z0[i][d + 1].wait_recv()
            zi = me.zz(sign * d)
            if d == FAR - 1:
                add(self.acc.at[zi, me.y, 0, pl.ds(i * HALF, HALF), :], self.zr0h.at[i])
            else:
                add(self.acc.at[zi, me.y, 0], self.zr0f.at[d, i])
            self.z0[i][d].start()

    def z1step(self, d, h):
        me = self.me
        for i, sign in enumerate((1, -1)):
            self.z1[i][h][d + 1].wait_recv()
            zi = me.zz(sign * d)
            for yi in range(2 * h, 2 * h + 2):
                if d == FAR - 1:
                    add(self.acc.at[zi, yi, 1, pl.ds(i * HALF, HALF), :], self.zr1h.at[i, yi])
                else:
                    add(self.acc.at[zi, yi, 1], self.zr1f.at[d, i, yi])
            self.z1[i][h][d].start()

    def z1last(self):
        me = self.me
        for h in range(2):
            for i in range(2):
                self.z1[i][h][1].wait_recv()
            for yi in range(2 * h, 2 * h + 2):
                add(self.acc.at[me.z, yi, 1], self.zr1f.at[0, 0, yi], self.zr1f.at[0, 1, yi])
        for copy in self.y1:
            copy.start()

    def z0last(self):
        me = self.me
        for i in range(2):
            self.z0[i][1].wait_recv()
        add(self.acc.at[me.z, me.y, 0], self.zr0f.at[0, 0], self.zr0f.at[0, 1])

    def y1last(self):
        me = self.me
        self.cp.arrived(self.y1_slot, NY - 1)
        add(self.acc.at[me.z, me.y, 1], *[self.yr1.at[k] for k in range(NY - 1)])


def fold(x, op):
    return op(x.reshape(x.shape[0] // 8, 8, x.shape[1]), axis=0)


def span_rows(i):
    return pl.ds(pl.multiple_of(i * SPAN, SPAN), SPAN)


def tables_kernel(slot_ref, len_ref, seen, source, rows_ref, span_of):
    chip = lax.axis_index("rail") // NC

    def invert(i, _):
        span_of[slot_ref[i]] = i
        return 0

    lax.fori_loop(0, NSLOT, invert, 0, unroll=16)
    for s in range(SLOTS):
        def clear(i, _):
            source[s * NSLOT + i] = SLOTS * WT
            return 0

        lax.fori_loop(0, NSLOT, clear, 0, unroll=32)

    row = lax.broadcasted_iota(jnp.int32, (8, LANES), 0)
    span_rows_ = jnp.zeros((8, LANES), jnp.int32)
    for s in range(SLOTS):
        span = span_of[chip * SLOTS + s]
        span_rows_ = jnp.where(row == s, span, span_rows_)
        for w in range(WT):
            n = span - (WT - 1) + w
            j = slot_ref[jnp.maximum(n, 0)]
            j = (j & ~15) | ((j & 3) << 2) | ((j >> 2) & 3)
            seen[s * WT + w] = j
            source[jnp.where(n >= 0, s * NSLOT + j, SLOTS * NSLOT)] = s * WT + w
    lane = lax.broadcasted_iota(jnp.int32, (8, LANES), 1) % SPAN
    qpos = span_rows_ * SPAN + lane
    qstart = jnp.zeros((8, LANES), jnp.int32)
    end = 0
    for i in range(len_ref.shape[0]):
        end = end + len_ref[i]
        qstart = jnp.where(qpos >= end, end, qstart)
    rows_ref[0] = qstart - (span_rows_ - (WT - 1)) * SPAN
    rows_ref[1] = qpos - qstart


def kernel(seen, source, rows_ref, q_ref, o_ref, k_ref, v_ref, dq_ref, dk_ref, dv_ref,
           k_all, v_all, qm, om, qs, os_, ot, tq, s_scr, p_scr, wk, wv, inv_scr, dqm,
           *rest):
    bufs_v, bufs_k = rest[:9], rest[9:18]
    send, recv, local = rest[18:]
    me = Place()
    cp = Copies(send, recv, k_all)
    x, z, y, c = me.x, me.z, me.y, me.c
    j_me = x * NC + c

    def cols(j, n):
        return pl.ds(pl.multiple_of(j * n, n), n)

    kvx = [[], []]
    own = []
    mine = pl.ds(pl.multiple_of((x % 2) * ROWS, ROWS), ROWS)
    kvx_slot = [cp.slot(), cp.slot()]
    for i, (src, dst) in enumerate(((k_ref, k_all), (v_ref, v_all))):
        for step in range(1, NX):
            to = (x + step) % NX
            kvx[i].append(cp.make(
                src.at[:, cols(to, HEAD)], dst.at[line(z, c, x // 2) + y, mine, :], me.at(x=to),
                0, kvx_slot[i]))
        own.append(pltpu.make_async_copy(
            src.at[:, cols(x, HEAD)], dst.at[line(z, c, x // 2) + y, mine, :], local.at[i]))
    rows = pl.ds(pl.multiple_of(c * BLOCK + x * ROWS, ROWS), ROWS)
    qo = [[], []]
    qo_slot = [cp.slot(), cp.slot()]
    for i, (src, dst) in enumerate(((q_ref, qm), (o_ref, om))):
        for j, dev in me.team():
            qo[i].append(cp.make(
                src.at[:, cols(j, WIDE)], dst.at[rows, :], dev, 0, qo_slot[i]))
        own.append(pltpu.make_async_copy(
            src.at[:, cols(j_me, WIDE)], dst.at[rows, :], local.at[2 + i]))
    gk, gv = Gather(me, cp, k_all, 1), Gather(me, cp, v_all, 2)
    sv = Scatter(me, cp, wv, source, bufs_v, 3)
    sk = Scatter(me, cp, wk, source, bufs_k, 4)
    dqs = []
    dqs_slot = cp.slot()
    for j, dev in me.team():
        there = pl.ds(pl.multiple_of((j % NC) * BLOCK + (j // NC) * ROWS, ROWS), ROWS)
        dqs.append(cp.make(
            dqm.at[there, :], dq_ref.at[:, cols(j_me, WIDE)], dev, 0, dqs_slot))
    own.append(pltpu.make_async_copy(dqm.at[rows, :], dq_ref.at[:, cols(j_me, WIDE)], local.at[4]))
    back = [[], []]
    back_slot = [cp.slot(), cp.slot()]
    for i, (acc, dst) in enumerate(((bufs_k[0], dk_ref), (bufs_v[0], dv_ref))):
        for step in range(1, NX):
            to = (x + step) % NX
            part = pl.ds(pl.multiple_of((to % 2) * ROWS, ROWS), ROWS)
            back[i].append(cp.make(
                acc.at[z, y, to // 2, part, :], dst.at[:, cols(x, HEAD)], me.at(x=to),
                0, back_slot[i]))
        own.append(pltpu.make_async_copy(
            acc.at[z, y, x // 2, mine, :], dst.at[:, cols(x, HEAD)], local.at[5 + i]))
    assert cp.count <= N_RECV

    greet(me)
    for i in range(2):
        for copy in kvx[i]:
            copy.start()
        own[i].start()
    cp.arrived(kvx_slot[0], NX - 1, ROWS)
    own[0].wait()
    gk.begin()
    for i in range(2):
        for copy in qo[i]:
            copy.start()
        own[2 + i].start()
    gk.near(1)
    gk.second()
    gk.finish(0)
    gk.near(2)
    gk.finish(-1)
    gk.wide(1, 0)
    gk.finish(1)
    gk.wide(1, 1)
    cp.arrived(kvx_slot[1], NX - 1, ROWS)
    own[1].wait()
    gv.begin()
    gk.near(3)
    gk.finish(-2)
    gk.wide(2, 0)
    gk.finish(2)
    gk.wide(2, 1)
    gv.near(1)
    gv.second()
    gk.near(4)
    gv.finish(0)
    gk.wide(3, 0)
    gk.finish(-3)
    gk.wide(3, 1)
    gk.finish(3)
    gv.near(2)
    gv.wide(1, 0)
    gv.finish(-1)
    gv.wide(1, 1)
    gv.finish(1)
    gk.wide(4, 0)
    gk.wide(4, 1)
    gk.finish(4)
    gv.near(3)
    gv.finish(-2)
    gv.wide(2, 0)
    gk.done()
    for i in range(2):
        cp.arrived(qo_slot[i], 14)
        own[2 + i].wait()

    sub = lax.broadcasted_iota(jnp.int32, (SPAN, 1), 0)
    wk[SLOTS * WT] = jnp.zeros((SPAN, HEAD), BF16)
    wv[SLOTS * WT] = jnp.zeros((SPAN, HEAD), BF16)
    mid = WT // 2

    def during(s, table):
        for i, events in enumerate(table):
            if events:
                @pl.when(s == i)
                def _():
                    for event in events:
                        event()

    def dv_tile(s, t):
        dv = jnp.dot(p_scr[s, t], os_[s], preferred_element_type=F32)
        wv[s * WT + t] = dv.astype(BF16)

    def first_part(s, _):
        low, extra = rows_ref[0, pl.ds(s, 1), :], rows_ref[1, pl.ds(s, 1), :]
        before = jnp.maximum(s - 1, 0)
        for h in range(QHEADS):
            qh = qm[span_rows(s), h * HEAD:(h + 1) * HEAD]
            qs[s, h * SPAN:(h + 1) * SPAN, :] = qh
            tq[:, h * SPAN:(h + 1) * SPAN] = qh.T
        top = jnp.full((8, LANES), NEG, F32)
        for t in range(WT):
            if t == mid:
                during(s, v_events[0])
            st = jnp.dot(k_all[seen[s * WT + t]], tq[...], preferred_element_type=F32)
            rel = (sub + t * SPAN) - low
            st = jnp.where((rel >= 0) & (rel <= extra), st, NEG)
            s_scr[t] = st
            top = jnp.maximum(top, fold(st, jnp.max))
        during(s, v_events[1])
        mc = jnp.max(top, axis=0, keepdims=True) * C2
        total = jnp.zeros((8, LANES), F32)
        for t in range(WT):
            if t == mid:
                during(s, v_events[2])
            dv_tile(before, t)
            p = jnp.exp2(s_scr[t] * C2 - mc)
            p_scr[s, t] = p.astype(BF16)
            total = total + fold(p, jnp.sum)
        inv = 1.0 / jnp.sum(total, axis=0, keepdims=True)
        inv8 = jnp.broadcast_to(inv, (8, LANES))
        inv_scr[s] = inv8
        for h in range(QHEADS):
            col = inv8[:, h * SPAN:(h + 1) * SPAN].T[:, :1]
            oh = om[span_rows(s), h * HEAD:(h + 1) * HEAD].astype(F32)
            oh = (oh * col).astype(BF16)
            os_[s, h * SPAN:(h + 1) * SPAN, :] = oh
            ot[s, :, h * SPAN:(h + 1) * SPAN] = oh.T
        during(s, v_events[3])
        return 0

    v_events = [
        [
            [lambda: gv.finish(2)],
            [lambda: gv.wide(3, 0), lambda: gv.finish(3)],
            [lambda: gv.wide(3, 1)],
            [lambda: gv.wide(4, 0)],
        ],
        [
            [lambda: gv.wide(2, 1)],
            None,
            [lambda: gv.finish(4)],
            None,
        ],
        [
            [lambda: gv.near(4)],
            None,
            None,
            None,
        ],
        [
            [lambda: gv.finish(-3)],
            None,
            None,
            [lambda: gv.wide(4, 1)],
        ],
    ]
    lax.fori_loop(0, SLOTS, first_part, 0)
    for t in range(WT):
        dv_tile(SLOTS - 1, t)

    sv.collect(4)
    sv.collect(3)
    sv.collect(-3)
    gv.done()
    sv.collect(2)
    sv.collect(-2)
    sv.collect(1)
    sv.pair(4)
    sv.collect(-1)
    sv.collect(0)
    sv.pair(3)

    def second_part(s, _):
        total = jnp.zeros((8, LANES), F32)
        for t in range(WT):
            if t == mid:
                during(s, k_events[0])
            dp = jnp.dot(v_all[seen[s * WT + t]], ot[s], preferred_element_type=F32)
            s_scr[t] = dp
            total = total + fold(p_scr[s, t].astype(F32) * dp, jnp.sum)
        during(s, k_events[1])
        dots = jnp.sum(total, axis=0, keepdims=True) * inv_scr[s, :1, :]
        for t in range(WT):
            if t == mid:
                during(s, k_events[2])
            ds = (p_scr[s, t].astype(F32) * (s_scr[t] - dots)).astype(BF16)
            p_scr[s, t] = ds
            dk = jnp.dot(ds, qs[s], preferred_element_type=F32) * SCALE
            wk[s * WT + t] = dk.astype(BF16)
        during(s, k_events[3])
        return 0

    def third_part(s, _):
        total = jnp.zeros((HEAD, LANES), F32)
        for t in range(WT):
            total = total + lax.dot_general(k_all[seen[s * WT + t]], p_scr[s, t],
                                            (((0,), (0,)), ((), ())), preferred_element_type=F32)
        for h in range(QHEADS):
            dqm[span_rows(s), h * HEAD:(h + 1) * HEAD] = (
                (total[:, h * SPAN:(h + 1) * SPAN] * SCALE).T.astype(BF16))
        during(s, q_events)
        return 0

    k_events = [
        [
            [lambda: sv.pair(-3)],
            [lambda: sv.pair(1)],
            None,
            [lambda: sv.yadd(-2)],
        ],
        [
            None,
            [lambda: sv.yadd(3)],
            [lambda: sv.z1step(2, 1), lambda: sv.z0step(3), lambda: sv.yadd(2)],
            None,
        ],
        [
            [lambda: sv.z1step(3, 0), lambda: sv.pair(2)],
            [lambda: sv.pair(-1)],
            None,
            [lambda: sv.z1step(1, 0)],
        ],
        [
            [lambda: sv.z1step(3, 1), lambda: sv.pair(-2), lambda: sv.yadd(4)],
            [lambda: sv.z1step(2, 0), lambda: sv.yadd(-3), lambda: sv.pair(0)],
            None,
            None,
        ],
    ]
    lax.fori_loop(0, SLOTS, second_part, 0)

    sk.collect(4)
    sk.collect(3)
    sk.collect(-3)
    sk.collect(2)
    sk.collect(-2)
    sk.collect(1)
    sk.pair(4)
    sk.collect(-1)
    sk.collect(0)
    sk.pair(3)
    sv.z0step(2)
    sv.z1step(1, 1)
    sv.yadd(1)
    sk.pair(-3)
    sv.yadd(-1)
    sv.yadd(0)
    q_events = [
        [lambda: sk.z1step(3, 0), lambda: sk.pair(2), lambda: sk.z1step(3, 1)],
        [lambda: sk.yadd(4), lambda: sk.pair(-2), lambda: sk.pair(1), lambda: sv.z0step(1)],
        [lambda: sk.yadd(3), lambda: sk.pair(-1), lambda: sv.z1last()],
        None,
    ]
    lax.fori_loop(0, SLOTS, third_part, 0)
    for copy in dqs:
        copy.start()
    own[4].start()
    sk.z1step(2, 0)
    sk.yadd(-3)
    sk.pair(0)
    sk.yadd(2)
    sk.z1step(2, 1)
    sk.z0step(3)
    sv.z0last()
    sk.yadd(-2)
    gk.drain()
    sk.yadd(1)
    sk.z1step(1, 0)
    sk.yadd(-1)
    sk.z1step(1, 1)
    sk.z0step(2)
    sv.y1last()
    for copy in back[1]:
        copy.start()
    own[6].start()
    sk.yadd(0)
    gv.drain()
    sk.z1last()
    sk.z0step(1)
    sv.drain()
    sk.z0last()
    sk.y1last()
    for copy in back[0]:
        copy.start()
    own[5].start()
    sk.drain()
    cp.arrived(dqs_slot, 14)
    for i in range(2):
        cp.arrived(back_slot[i], NX - 1, ROWS)
    cp.sent(0, 48)
    for i in (4, 5, 6):
        own[i].wait()


def settle_kernel(dq_in, dk_in, dv_in, dq_out, dk_out, dv_out):
    dq_out[...] = dq_in[...]
    dk_out[...] = dk_in[...]
    dv_out[...] = dv_in[...]


def per_device(queries, keys, values, output_cotangent, doc_lengths, span_slot):
    smem = pl.BlockSpec(memory_space=pltpu.SMEM)
    any_spec = pl.BlockSpec(memory_space=pl.ANY)

    def vmem(*shape, dtype=BF16):
        return pltpu.VMEM(shape, dtype)

    scatter_bufs = [
        vmem(NZ, NY, 2, SPAN, HEAD),
        vmem(NZ, NY, 2, SPAN, HEAD),
        vmem(NZ, NY, 2, SPAN, HEAD),
        vmem(NZ, NY - 1, SPAN, HEAD),
        vmem(NY - 1, SPAN, HEAD),
        vmem(2, HALF, HEAD),
        vmem(FAR - 1, 2, SPAN, HEAD),
        vmem(2, NY, HALF, HEAD),
        vmem(FAR - 1, 2, NY, SPAN, HEAD),
    ]
    seen, source, rows = pl.pallas_call(
        tables_kernel,
        out_shape=[
            jax.ShapeDtypeStruct((SLOTS * WT,), jnp.int32),
            jax.ShapeDtypeStruct((SLOTS * NSLOT + 8,), jnp.int32),
            jax.ShapeDtypeStruct((2, 8, LANES), jnp.int32),
        ],
        in_specs=[smem] * 2,
        out_specs=[smem, smem, pl.BlockSpec(memory_space=pltpu.VMEM)],
        scratch_shapes=[pltpu.SMEM((NSLOT,), jnp.int32)],
        name="tables",
    )(span_slot, doc_lengths)
    outs = pl.pallas_call(
        kernel,
        out_shape=[
            jax.ShapeDtypeStruct(queries.shape, BF16),
            jax.ShapeDtypeStruct(keys.shape, BF16),
            jax.ShapeDtypeStruct(values.shape, BF16),
        ],
        in_specs=[smem] * 2 + [pl.BlockSpec(memory_space=pltpu.VMEM)] + [any_spec] * 4,
        out_specs=[any_spec] * 3,
        scratch_shapes=[
            vmem(NSLOT, SPAN, HEAD),
            vmem(NSLOT, SPAN, HEAD),
            vmem(SLOTS * SPAN, WIDE),
            vmem(SLOTS * SPAN, WIDE),
            vmem(SLOTS, LANES, HEAD),
            vmem(SLOTS, LANES, HEAD),
            vmem(SLOTS, HEAD, LANES),
            vmem(HEAD, LANES),
            vmem(WT, SPAN, LANES, dtype=F32),
            vmem(SLOTS, WT, SPAN, LANES),
            vmem(SLOTS * WT + 1, SPAN, HEAD),
            vmem(SLOTS * WT + 1, SPAN, HEAD),
            vmem(SLOTS, 8, LANES, dtype=F32),
            vmem(SLOTS * SPAN, WIDE),
        ] + scatter_bufs * 2 + [
            pltpu.SemaphoreType.DMA((N_SEND,)),
            pltpu.SemaphoreType.DMA((N_RECV,)),
            pltpu.SemaphoreType.DMA((8,)),
        ],
        compiler_params=pltpu.CompilerParams(
            collective_id=0, has_side_effects=True, vmem_limit_bytes=60 * 1024 * 1024),
        name="attention_backward",
    )(seen, source, rows, queries, output_cotangent, keys, values)
    outs = pl.pallas_call(
        settle_kernel,
        out_shape=[jax.ShapeDtypeStruct(out.shape, out.dtype) for out in outs],
        in_specs=[pl.BlockSpec(memory_space=pltpu.VMEM)] * 3,
        out_specs=[pl.BlockSpec(memory_space=pltpu.VMEM)] * 3,
        name="settle",
    )(*outs)
    return tuple(outs)


def solution(mesh):
    rows = P(("rail", "node"), None)
    return jax.shard_map(
        per_device, mesh=mesh, in_specs=(rows, rows, rows, rows, P(), P()),
        out_specs=(rows, rows, rows), check_vma=False,
    )
```

```python
import math

import jax
import jax.numpy as jnp
from jax import lax
from jax.experimental import pallas as pl
from jax.experimental.pallas import tpu as pltpu
from jax.sharding import PartitionSpec as P

HEAD = 128
SPAN = 128
NX, NZ, NY, NC = 4, 8, 4, 2
ROWS = 64
BLOCK = NX * ROWS
SLOTS = 4
NSLOT = NZ * NY * SLOTS
QHEADS = 4
LANES = QHEADS * SPAN
WIDE = QHEADS * HEAD
WT = 17
PAD = WT + 2
HALF = SPAN // 2
FAR = NZ // 2
SCALE = 1.0 / math.sqrt(HEAD)
C2 = SCALE * 1.4426950408889634
NEG = -1e30
MESH = pl.DeviceIdType.MESH
F32 = jnp.float32
BF16 = jnp.bfloat16
N_RECV = 208
N_SEND = 5
RULER = 126
COLUMNS = [0, 1, -1, 2, -2, 3, -3, 4]


class Place:
    def __init__(self):
        self.x = lax.axis_index("node")
        rail = lax.axis_index("rail")
        self.c = rail % NC
        self.y = (rail // NC) % NY
        self.z = rail // (NC * NY)

    def at(self, x=None, z=None, y=None, c=None):
        x = self.x if x is None else x
        z = self.z if z is None else z
        y = self.y if y is None else y
        c = self.c if c is None else c
        return (x, (z * NY + y) * NC + c)

    def zz(self, d):
        return (self.z + d + NZ) % NZ

    def yy(self, d):
        return (self.y + d + NY) % NY

    def ring(self, axis, step):
        return self.at(z=self.zz(step)) if axis == "z" else self.at(y=self.yy(step))

    def sibling(self):
        return self.at(c=1 - self.c)

    def team(self):
        out = []
        for step in range(1, NX * NC):
            j = (self.x * NC + self.c + step) % (NX * NC)
            out.append((j, self.at(x=j // NC, c=j % NC)))
        return out


def greet(place):
    barrier = pltpu.get_barrier_semaphore()
    peers = [dev for _, dev in place.team()]
    peers += [place.ring("z", 1), place.ring("z", -1)]
    peers += [place.ring("y", k) for k in range(1, NY)]
    for dev in peers:
        pl.semaphore_signal(barrier, inc=1, device_id=dev, device_id_type=MESH)
    pl.semaphore_wait(barrier, len(peers))


class Copies:
    def __init__(self, send, recv, ruler):
        self.send, self.recv, self.ruler, self.count = send, recv, ruler, 0

    def slot(self):
        self.count += 1
        return self.count - 1

    def make(self, src, dst, dev, group, slot=None):
        slot = self.slot() if slot is None else slot
        return pltpu.make_async_remote_copy(
            src_ref=src, dst_ref=dst, send_sem=self.send.at[group], recv_sem=self.recv.at[slot],
            device_id=dev, device_id_type=MESH,
        )

    def size(self, spans, rows=SPAN):
        return self.ruler.at[pl.ds(0, spans), pl.ds(0, rows), :]

    def arrived(self, slot, spans, rows=SPAN):
        ref = self.size(spans, rows)
        pltpu.make_async_copy(ref, ref, self.recv.at[slot]).wait()

    def sent(self, group, spans):
        ref = self.size(spans)
        pltpu.make_async_copy(ref, ref, self.send.at[group]).wait()


def line(z, c, b):
    return ((z * NC + c) * 2 + b) * NY


class Gather:
    def __init__(self, me, cp, ref, group):
        self.cp, self.ref, self.group = cp, ref, group
        c, y = me.c, me.y

        def blk(zi, yi, b, lo=0, n=SPAN):
            return ref.at[line(zi, c, b) + yi, pl.ds(lo, n), :]

        def make(src, dev, slot=None):
            return cp.make(src, src, dev, group, slot)

        self.z = [{}, {}]
        self.z2 = [[{} for _ in range(NY)] for _ in range(2)]
        for d in range(1, FAR + 1):
            for i, sign in enumerate((1, -1)):
                lo, n = (i * HALF, HALF) if d == FAR else (0, SPAN)
                zi = me.zz(-sign * (d - 1))
                to = me.ring("z", sign)
                self.z[i][d] = make(blk(zi, y, 0, lo, n), to)
                for k in range(NY):
                    self.z2[i][k][d] = make(blk(zi, me.yy(k), 1, lo, n), to)
        self.y, self.y_slot = {}, {}
        for d in COLUMNS:
            self.y_slot[d] = cp.slot()
            src = blk(me.zz(d), y, 0)
            self.y[d] = [make(src, me.ring("y", k), self.y_slot[d]) for k in range(1, NY)]
        src = blk(me.z, y, 1)
        self.y2 = [make(src, me.ring("y", k)) for k in range(1, NY)]
        self.sib = [{}, {}]
        self.sib_slot = cp.slot()
        for d in COLUMNS:
            for b in range(2):
                src = ref.at[pl.ds(line(me.zz(d), c, b), NY)]
                self.sib[b][d] = make(src, me.sibling(), self.sib_slot)

    def begin(self):
        for i in range(2):
            self.z[i][1].start()
        for copy in self.y2:
            copy.start()
        for i in range(2):
            self.z2[i][0][1].start()
        for copy in self.y[0]:
            copy.start()

    def second(self):
        for k in range(1, NY):
            self.y2[k - 1].wait_recv()
            for i in range(2):
                self.z2[i][NY - k][1].start()
        self.sib[1][0].start()

    def near(self, d):
        for i, sign in enumerate((1, -1)):
            self.z[i][d].wait_recv()
            if d < FAR:
                self.z[i][d + 1].start()
                for copy in self.y[-sign * d]:
                    copy.start()
        if d == FAR:
            for copy in self.y[FAR]:
                copy.start()

    def wide(self, d, half):
        for k in ((0, 3), (2, 1))[half]:
            for i in range(2):
                self.z2[i][k][d].wait_recv()
                if d < FAR:
                    self.z2[i][k][d + 1].start()
        if half:
            self.sib[1][d].start()
            if d < FAR:
                self.sib[1][-d].start()

    def finish(self, *cols):
        for d in cols:
            self.cp.arrived(self.y_slot[d], NY - 1)
            self.sib[0][d].start()

    def done(self):
        self.cp.arrived(self.sib_slot, NSLOT // 2)

    def drain(self):
        self.cp.sent(self.group, RULER)


def add(dst, *srcs):
    if len(srcs) == 1:
        dst[...] += srcs[0][...]
        return
    total = dst[...].astype(F32)
    for src in srcs:
        total = total + src[...].astype(F32)
    dst[...] = total.astype(BF16)


class Scatter:
    def __init__(self, me, cp, window, source, bufs, group):
        self.me, self.cp, self.window, self.source, self.group = me, cp, window, source, group
        (self.acc, self.snd, self.sibr, self.yr, self.yr1,
         self.zr0h, self.zr0f, self.zr1h, self.zr1f) = bufs
        acc, y = self.acc, me.y
        self.sib, self.y0, self.y0_slot = {}, {}, {}

        def make(src, dst, dev, slot=None):
            return cp.make(src, dst, dev, group, slot)

        for i, d in enumerate(COLUMNS):
            self.sib[d] = make(self.snd.at[me.zz(d)], self.sibr.at[me.zz(d)], me.sibling())
            self.y0_slot[d] = cp.slot()
            self.y0[d] = [
                make(acc.at[me.zz(d), me.yy(k), 0], self.yr.at[i, k - 1], me.ring("y", k),
                     self.y0_slot[d])
                for k in range(1, NY)
            ]
        self.y1_slot = cp.slot()
        self.y1 = [
            make(acc.at[me.z, me.yy(k), 1], self.yr1.at[k - 1], me.ring("y", k), self.y1_slot)
            for k in range(1, NY)
        ]
        self.z0 = [{}, {}]
        self.z1 = [[{}, {}], [{}, {}]]
        for d in range(FAR, 0, -1):
            for i, sign in enumerate((1, -1)):
                to = me.ring("z", sign)
                zi = me.zz(sign * d)
                rows = pl.ds(i * HALF, HALF) if d == FAR else pl.ds(0, SPAN)
                dst = self.zr0h.at[i] if d == FAR else self.zr0f.at[d - 1, i]
                self.z0[i][d] = make(acc.at[zi, y, 0, rows, :], dst, to)
                for h in range(2):
                    ys = pl.ds(2 * h, 2)
                    dst = self.zr1h.at[i, ys] if d == FAR else self.zr1f.at[d - 1, i, ys]
                    self.z1[i][h][d] = make(acc.at[zi, ys, 1, rows, :], dst, to)

    def drain(self):
        self.cp.sent(self.group, RULER)

    def collect(self, d):
        me = self.me
        zi = me.zz(d)

        def tiles(core, dst):
            def body(i, _):
                yi, b = i // 2, i % 2
                j = line(zi, core, b) + yi
                total = None
                for s in range(SLOTS):
                    w = self.source[s * NSLOT + j]
                    tile = self.window[w]
                    total = tile if total is None else total + tile
                dst[zi, yi, b] = total
                return 0
            lax.fori_loop(0, NY * 2, body, 0, unroll=8)

        tiles(1 - me.c, self.snd)
        self.sib[d].start()
        tiles(me.c, self.acc)

    def pair(self, *cols):
        me = self.me
        for d in cols:
            zi = me.zz(d)
            self.sib[d].wait_recv()

            add(self.acc.at[zi], self.sibr.at[zi])
            for copy in self.y0[d]:
                copy.start()
            if d == FAR:
                for h in range(2):
                    for i in range(2):
                        self.z1[i][h][d].start()

    def yadd(self, *cols):
        me = self.me
        for d in cols:
            j = COLUMNS.index(d)
            self.cp.arrived(self.y0_slot[d], NY - 1)
            add(self.acc.at[me.zz(d), me.y, 0], *[self.yr.at[j, k] for k in range(NY - 1)])
            if d == FAR:
                for i in range(2):
                    self.z0[i][d].start()

    def z0step(self, d):
        me = self.me
        for i, sign in enumerate((1, -1)):
            self.z0[i][d + 1].wait_recv()
            zi = me.zz(sign * d)
            if d == FAR - 1:
                add(self.acc.at[zi, me.y, 0, pl.ds(i * HALF, HALF), :], self.zr0h.at[i])
            else:
                add(self.acc.at[zi, me.y, 0], self.zr0f.at[d, i])
            self.z0[i][d].start()

    def z1step(self, d, h):
        me = self.me
        for i, sign in enumerate((1, -1)):
            self.z1[i][h][d + 1].wait_recv()
            zi = me.zz(sign * d)
            for yi in range(2 * h, 2 * h + 2):
                if d == FAR - 1:
                    add(self.acc.at[zi, yi, 1, pl.ds(i * HALF, HALF), :], self.zr1h.at[i, yi])
                else:
                    add(self.acc.at[zi, yi, 1], self.zr1f.at[d, i, yi])
            self.z1[i][h][d].start()

    def z1last(self):
        me = self.me
        for h in range(2):
            for i in range(2):
                self.z1[i][h][1].wait_recv()
            for yi in range(2 * h, 2 * h + 2):
                add(self.acc.at[me.z, yi, 1], self.zr1f.at[0, 0, yi], self.zr1f.at[0, 1, yi])
        for copy in self.y1:
            copy.start()

    def z0last(self):
        me = self.me
        for i in range(2):
            self.z0[i][1].wait_recv()
        add(self.acc.at[me.z, me.y, 0], self.zr0f.at[0, 0], self.zr0f.at[0, 1])

    def y1last(self):
        me = self.me
        self.cp.arrived(self.y1_slot, NY - 1)
        add(self.acc.at[me.z, me.y, 1], *[self.yr1.at[k] for k in range(NY - 1)])


def fold(x, op):
    return op(x.reshape(x.shape[0] // 8, 8, x.shape[1]), axis=0)


def span_rows(i):
    return pl.ds(pl.multiple_of(i * SPAN, SPAN), SPAN)


def swap_fields(j):
    return (j & ~15) | ((j & 3) << 2) | ((j >> 2) & 3)


def make_tables(chip, slot_ref, slot_row, len_ref, seen, source, rows_scr):
    numbers = lax.broadcasted_iota(jnp.int32, (1, NSLOT), 1)
    slots = slot_row[...]

    def span_in(j):
        return jnp.sum(jnp.where(slots == j, numbers, 0))

    spans = [span_in(chip * SLOTS + s) for s in range(SLOTS)]
    row = lax.broadcasted_iota(jnp.int32, (8, LANES), 0)
    base = jnp.zeros((8, LANES), jnp.int32)
    for s in range(SLOTS):
        base = jnp.where(row == s, spans[s], base)
        for w in range(WT):
            n = jnp.clip(spans[s] + (w - (WT - 1)), 0, NSLOT - 1)
            seen[s * WT + w] = swap_fields(slot_ref[n])
    qpos = base * SPAN + lax.broadcasted_iota(jnp.int32, (8, LANES), 1) % SPAN
    qstart = jnp.zeros((8, LANES), jnp.int32)
    end = 0
    for i in range(len_ref.shape[0]):
        end = end + len_ref[i]
        qstart = jnp.where(qpos >= end, end, qstart)
    rows_scr[0] = qstart - (base - (WT - 1)) * SPAN
    rows_scr[1] = qpos - qstart

    def fill(i, _):
        n = span_in(swap_fields(i))
        for s in range(SLOTS):
            t = jnp.minimum(jnp.maximum(n - spans[s] + WT, 0), WT + 1)
            source[s * NSLOT + i] = s * PAD + t
        return 0

    lax.fori_loop(0, NSLOT, fill, 0, unroll=8)


def kernel(slot_ref, len_ref, slot_row, q_ref, o_ref, k_ref, v_ref, dq_ref, dk_ref, dv_ref,
           k_all, v_all, qm, om, qs, os_, ot, tq, s_scr, p_scr, wk, wv, inv_scr, dqm, seen, source, rows_ref,
           *rest):
    bufs_v, bufs_k = rest[:9], rest[9:18]
    send, recv, local = rest[18:]
    me = Place()
    cp = Copies(send, recv, k_all)
    x, z, y, c = me.x, me.z, me.y, me.c
    j_me = x * NC + c

    def cols(j, n):
        return pl.ds(pl.multiple_of(j * n, n), n)

    kvx = [[], []]
    own = []
    mine = pl.ds(pl.multiple_of((x % 2) * ROWS, ROWS), ROWS)
    kvx_slot = [cp.slot(), cp.slot()]
    for i, (src, dst) in enumerate(((k_ref, k_all), (v_ref, v_all))):
        for step in range(1, NX):
            to = (x + step) % NX
            kvx[i].append(cp.make(
                src.at[:, cols(to, HEAD)], dst.at[line(z, c, x // 2) + y, mine, :], me.at(x=to),
                0, kvx_slot[i]))
        own.append(pltpu.make_async_copy(
            src.at[:, cols(x, HEAD)], dst.at[line(z, c, x // 2) + y, mine, :], local.at[i]))
    rows = pl.ds(pl.multiple_of(c * BLOCK + x * ROWS, ROWS), ROWS)
    qo = [[], []]
    qo_slot = [cp.slot(), cp.slot()]
    for i, (src, dst) in enumerate(((q_ref, qm), (o_ref, om))):
        for j, dev in me.team():
            qo[i].append(cp.make(
                src.at[:, cols(j, WIDE)], dst.at[rows, :], dev, 0, qo_slot[i]))
        own.append(pltpu.make_async_copy(
            src.at[:, cols(j_me, WIDE)], dst.at[rows, :], local.at[2 + i]))
    gk, gv = Gather(me, cp, k_all, 1), Gather(me, cp, v_all, 2)
    sv = Scatter(me, cp, wv, source, bufs_v, 3)
    sk = Scatter(me, cp, wk, source, bufs_k, 4)
    dqs = []
    dqs_slot = cp.slot()
    for j, dev in me.team():
        there = pl.ds(pl.multiple_of((j % NC) * BLOCK + (j // NC) * ROWS, ROWS), ROWS)
        dqs.append(cp.make(
            dqm.at[there, :], dq_ref.at[:, cols(j_me, WIDE)], dev, 0, dqs_slot))
    own.append(pltpu.make_async_copy(dqm.at[rows, :], dq_ref.at[:, cols(j_me, WIDE)], local.at[4]))
    back = [[], []]
    back_slot = [cp.slot(), cp.slot()]
    for i, (acc, dst) in enumerate(((bufs_k[0], dk_ref), (bufs_v[0], dv_ref))):
        for step in range(1, NX):
            to = (x + step) % NX
            part = pl.ds(pl.multiple_of((to % 2) * ROWS, ROWS), ROWS)
            back[i].append(cp.make(
                acc.at[z, y, to // 2, part, :], dst.at[:, cols(x, HEAD)], me.at(x=to),
                0, back_slot[i]))
        own.append(pltpu.make_async_copy(
            acc.at[z, y, x // 2, mine, :], dst.at[:, cols(x, HEAD)], local.at[5 + i]))
    assert cp.count <= N_RECV

    greet(me)
    for i in range(2):
        for copy in kvx[i]:
            copy.start()
        own[i].start()
    cp.arrived(kvx_slot[0], NX - 1, ROWS)
    own[0].wait()
    gk.begin()
    for i in range(2):
        for copy in qo[i]:
            copy.start()
        own[2 + i].start()
    make_tables(z * NY + y, slot_ref, slot_row, len_ref, seen, source, rows_ref)
    gk.near(1)
    gk.second()
    gk.finish(0)
    gk.near(2)
    gk.finish(-1)
    gk.wide(1, 0)
    gk.finish(1)
    gk.wide(1, 1)
    cp.arrived(kvx_slot[1], NX - 1, ROWS)
    own[1].wait()
    gv.begin()
    gk.near(3)
    gk.finish(-2)
    gk.wide(2, 0)
    gk.finish(2)
    gk.wide(2, 1)
    gv.near(1)
    gv.second()
    gk.near(4)
    gv.finish(0)
    gk.wide(3, 0)
    gk.finish(-3)
    gk.wide(3, 1)
    gk.finish(3)
    gv.near(2)
    gv.wide(1, 0)
    gv.finish(-1)
    gv.wide(1, 1)
    gv.finish(1)
    gk.wide(4, 0)
    gk.wide(4, 1)
    gk.finish(4)
    gv.near(3)
    gv.finish(-2)
    gv.wide(2, 0)
    gk.done()
    for i in range(2):
        cp.arrived(qo_slot[i], 14)
        own[2 + i].wait()

    sub = lax.broadcasted_iota(jnp.int32, (SPAN, 1), 0)
    for s in range(SLOTS):
        for t in (0, WT + 1):
            wk[s * PAD + t] = jnp.zeros((SPAN, HEAD), BF16)
            wv[s * PAD + t] = jnp.zeros((SPAN, HEAD), BF16)
    mid = WT // 2

    def during(s, table):
        for i, events in enumerate(table):
            if events:
                @pl.when(s == i)
                def _():
                    for event in events:
                        event()

    def dv_tile(s, t):
        dv = jnp.dot(p_scr[s, t], os_[s], preferred_element_type=F32)
        wv[s * PAD + 1 + t] = dv.astype(BF16)

    def first_part(s, _):
        low, extra = rows_ref[0, pl.ds(s, 1), :], rows_ref[1, pl.ds(s, 1), :]
        before = jnp.maximum(s - 1, 0)
        for h in range(QHEADS):
            qh = qm[span_rows(s), h * HEAD:(h + 1) * HEAD]
            qs[s, h * SPAN:(h + 1) * SPAN, :] = qh
            tq[:, h * SPAN:(h + 1) * SPAN] = qh.T
        top = jnp.full((8, LANES), NEG, F32)
        for t in range(WT):
            if t == mid:
                during(s, v_events[0])
            st = jnp.dot(k_all[seen[s * WT + t]], tq[...], preferred_element_type=F32)
            rel = (sub + t * SPAN) - low
            st = jnp.where((rel >= 0) & (rel <= extra), st, NEG)
            s_scr[t] = st
            top = jnp.maximum(top, fold(st, jnp.max))
        during(s, v_events[1])
        mc = jnp.max(top, axis=0, keepdims=True) * C2
        total = jnp.zeros((8, LANES), F32)
        for t in range(WT):
            if t == mid:
                during(s, v_events[2])
            dv_tile(before, t)
            p = jnp.exp2(s_scr[t] * C2 - mc)
            p_scr[s, t] = p.astype(BF16)
            total = total + fold(p, jnp.sum)
        inv = 1.0 / jnp.sum(total, axis=0, keepdims=True)
        inv8 = jnp.broadcast_to(inv, (8, LANES))
        inv_scr[s] = inv8
        for h in range(QHEADS):
            col = inv8[:, h * SPAN:(h + 1) * SPAN].T[:, :1]
            oh = om[span_rows(s), h * HEAD:(h + 1) * HEAD].astype(F32)
            oh = (oh * col).astype(BF16)
            os_[s, h * SPAN:(h + 1) * SPAN, :] = oh
            ot[s, :, h * SPAN:(h + 1) * SPAN] = oh.T
        during(s, v_events[3])
        return 0

    v_events = [
        [
            [lambda: gv.finish(2)],
            [lambda: gv.wide(3, 0), lambda: gv.finish(3)],
            [lambda: gv.wide(3, 1)],
            [lambda: gv.wide(4, 0)],
        ],
        [
            [lambda: gv.wide(2, 1)],
            None,
            [lambda: gv.finish(4)],
            None,
        ],
        [
            [lambda: gv.near(4)],
            None,
            None,
            None,
        ],
        [
            [lambda: gv.finish(-3)],
            None,
            None,
            [lambda: gv.wide(4, 1)],
        ],
    ]
    lax.fori_loop(0, SLOTS, first_part, 0)
    for t in range(WT):
        dv_tile(SLOTS - 1, t)

    sv.collect(4)
    sv.collect(3)
    sv.collect(-3)
    gv.done()
    sv.collect(2)
    sv.collect(-2)
    sv.collect(1)
    sv.pair(4)
    sv.collect(-1)
    sv.collect(0)
    sv.pair(3)

    def second_part(s, _):
        total = jnp.zeros((8, LANES), F32)
        for t in range(WT):
            if t == mid:
                during(s, k_events[0])
            dp = jnp.dot(v_all[seen[s * WT + t]], ot[s], preferred_element_type=F32)
            s_scr[t] = dp
            total = total + fold(p_scr[s, t].astype(F32) * dp, jnp.sum)
        during(s, k_events[1])
        dots = jnp.sum(total, axis=0, keepdims=True) * inv_scr[s, :1, :]
        for t in range(WT):
            if t == mid:
                during(s, k_events[2])
            ds = (p_scr[s, t].astype(F32) * (s_scr[t] - dots)).astype(BF16)
            p_scr[s, t] = ds
            dk = jnp.dot(ds, qs[s], preferred_element_type=F32) * SCALE
            wk[s * PAD + 1 + t] = dk.astype(BF16)
        during(s, k_events[3])
        return 0

    def third_part(s, _):
        total = jnp.zeros((HEAD, LANES), F32)
        for t in range(WT):
            total = total + lax.dot_general(k_all[seen[s * WT + t]], p_scr[s, t],
                                            (((0,), (0,)), ((), ())), preferred_element_type=F32)
        for h in range(QHEADS):
            dqm[span_rows(s), h * HEAD:(h + 1) * HEAD] = (
                (total[:, h * SPAN:(h + 1) * SPAN] * SCALE).T.astype(BF16))
        during(s, q_events)
        return 0

    k_events = [
        [
            [lambda: sv.pair(-3)],
            [lambda: sv.pair(1)],
            None,
            [lambda: sv.yadd(-2)],
        ],
        [
            None,
            [lambda: sv.yadd(3)],
            [lambda: sv.z1step(2, 1), lambda: sv.z0step(3), lambda: sv.yadd(2)],
            None,
        ],
        [
            [lambda: sv.z1step(3, 0), lambda: sv.pair(2)],
            [lambda: sv.pair(-1)],
            None,
            [lambda: sv.z1step(1, 0)],
        ],
        [
            [lambda: sv.z1step(3, 1), lambda: sv.pair(-2), lambda: sv.yadd(4)],
            [lambda: sv.z1step(2, 0), lambda: sv.yadd(-3), lambda: sv.pair(0)],
            None,
            None,
        ],
    ]
    lax.fori_loop(0, SLOTS, second_part, 0)

    sk.collect(4)
    sk.collect(3)
    sk.collect(-3)
    sk.collect(2)
    sk.collect(-2)
    sk.collect(1)
    sk.pair(4)
    sk.collect(-1)
    sk.collect(0)
    sk.pair(3)
    sv.z0step(2)
    sv.z1step(1, 1)
    sv.yadd(1)
    sk.pair(-3)
    sv.yadd(-1)
    sv.yadd(0)
    q_events = [
        [lambda: sk.z1step(3, 0), lambda: sk.pair(2), lambda: sk.z1step(3, 1)],
        [lambda: sk.yadd(4), lambda: sk.pair(-2), lambda: sk.pair(1), lambda: sv.z0step(1)],
        [lambda: sk.yadd(3), lambda: sk.pair(-1), lambda: sv.z1last()],
        None,
    ]
    lax.fori_loop(0, SLOTS, third_part, 0)
    for copy in dqs:
        copy.start()
    own[4].start()
    sk.z1step(2, 0)
    sk.yadd(-3)
    sk.pair(0)
    sk.yadd(2)
    sk.z1step(2, 1)
    sk.z0step(3)
    sv.z0last()
    sk.yadd(-2)
    gk.drain()
    sk.yadd(1)
    sk.z1step(1, 0)
    sk.yadd(-1)
    sk.z1step(1, 1)
    sk.z0step(2)
    sv.y1last()
    for copy in back[1]:
        copy.start()
    own[6].start()
    sk.yadd(0)
    gv.drain()
    sk.z1last()
    sk.z0step(1)
    sv.drain()
    sk.z0last()
    sk.y1last()
    for copy in back[0]:
        copy.start()
    own[5].start()
    sk.drain()
    cp.arrived(dqs_slot, 14)
    for i in range(2):
        cp.arrived(back_slot[i], NX - 1, ROWS)
    cp.sent(0, 48)
    for i in (4, 5, 6):
        own[i].wait()


def settle_kernel(dq_in, dk_in, dv_in, dq_out, dk_out, dv_out):
    dq_out[...] = dq_in[...]
    dk_out[...] = dk_in[...]
    dv_out[...] = dv_in[...]


def per_device(queries, keys, values, output_cotangent, doc_lengths, span_slot):
    smem = pl.BlockSpec(memory_space=pltpu.SMEM)
    any_spec = pl.BlockSpec(memory_space=pl.ANY)

    def vmem(*shape, dtype=BF16):
        return pltpu.VMEM(shape, dtype)

    scatter_bufs = [
        vmem(NZ, NY, 2, SPAN, HEAD),
        vmem(NZ, NY, 2, SPAN, HEAD),
        vmem(NZ, NY, 2, SPAN, HEAD),
        vmem(NZ, NY - 1, SPAN, HEAD),
        vmem(NY - 1, SPAN, HEAD),
        vmem(2, HALF, HEAD),
        vmem(FAR - 1, 2, SPAN, HEAD),
        vmem(2, NY, HALF, HEAD),
        vmem(FAR - 1, 2, NY, SPAN, HEAD),
    ]
    outs = pl.pallas_call(
        kernel,
        out_shape=[
            jax.ShapeDtypeStruct(queries.shape, BF16),
            jax.ShapeDtypeStruct(keys.shape, BF16),
            jax.ShapeDtypeStruct(values.shape, BF16),
        ],
        in_specs=[smem] * 2 + [pl.BlockSpec(memory_space=pltpu.VMEM)] + [any_spec] * 4,
        out_specs=[any_spec] * 3,
        scratch_shapes=[
            vmem(NSLOT, SPAN, HEAD),
            vmem(NSLOT, SPAN, HEAD),
            vmem(SLOTS * SPAN, WIDE),
            vmem(SLOTS * SPAN, WIDE),
            vmem(SLOTS, LANES, HEAD),
            vmem(SLOTS, LANES, HEAD),
            vmem(SLOTS, HEAD, LANES),
            vmem(HEAD, LANES),
            vmem(WT, SPAN, LANES, dtype=F32),
            vmem(SLOTS, WT, SPAN, LANES),
            vmem(SLOTS * PAD, SPAN, HEAD),
            vmem(SLOTS * PAD, SPAN, HEAD),
            vmem(SLOTS, 8, LANES, dtype=F32),
            vmem(SLOTS * SPAN, WIDE),
            pltpu.SMEM((SLOTS * WT,), jnp.int32),
            pltpu.SMEM((SLOTS * NSLOT,), jnp.int32),
            vmem(2, 8, LANES, dtype=jnp.int32),
        ] + scatter_bufs * 2 + [
            pltpu.SemaphoreType.DMA((N_SEND,)),
            pltpu.SemaphoreType.DMA((N_RECV,)),
            pltpu.SemaphoreType.DMA((8,)),
        ],
        compiler_params=pltpu.CompilerParams(
            collective_id=0, has_side_effects=True, vmem_limit_bytes=60 * 1024 * 1024),
        name="attention_backward",
    )(span_slot, doc_lengths, span_slot.reshape(1, NSLOT), queries, output_cotangent, keys, values)
    outs = pl.pallas_call(
        settle_kernel,
        out_shape=[jax.ShapeDtypeStruct(out.shape, out.dtype) for out in outs],
        in_specs=[pl.BlockSpec(memory_space=pltpu.VMEM)] * 3,
        out_specs=[pl.BlockSpec(memory_space=pltpu.VMEM)] * 3,
        name="settle",
    )(*outs)
    return tuple(outs)


def solution(mesh):
    rows = P(("rail", "node"), None)
    return jax.shard_map(
        per_device, mesh=mesh, in_specs=(rows, rows, rows, rows, P(), P()),
        out_specs=(rows, rows, rows), check_vma=False,
    )
```
